512 devices in a mesh: vocab: 64 (over z, x), tok: 8 (over y, core).
Axes of the slice: x: 4, y: 4, z: 16, core: 2. Of those that a mesh axis runs over, the one named last changes fastest.
Arguments:
- target_logits: bfloat16 [1024, 131072], P('tok', 'vocab'), may hold values from -250 to 250
- draft_hidden: bfloat16 [2, 1024, 4096], P(None, 'tok', 'vocab'), may hold values from -210 to 210
- draft_head: bfloat16 [32768, 4096], P('vocab'), may hold values from -0.375 to 0.375
- block_map: int32 [256], replicated, may hold values from 0 to 1023, as said below
Outputs:
- grad_hidden: bfloat16 [2, 1024, 4096], P(None, 'tok', 'vocab')
- per_token_loss: float32 [2, 1024], P(None, ('tok', 'vocab'))
The draws below stay inside these ranges and needn't reach their ends.
Inputs may be any that keep to these rules, and one draw needn't show every extreme that they name: block_map names 256 different target blocks; at most 8 of them lie among the 16 blocks of one vocab device, and exactly 8 on some device.
All inputs are finite; a program needn't handle non-finite values.
Results may differ from the reference program's by a relative error of at most 0.004.
The reference program's roundings to bfloat16 on the way count: a program that leaves them out, or rounds other values in their place, can miss the bound.
Values may be sent and summed in bfloat16 or wider, within the bound.
A program may use at most 64 MiB of HBM per device.

```python
import math
import jax
import jax.numpy as jnp
from jax import lax

D = 4096
BLK = 128
TBLK_DEV = 16
SEL_MAX = 8
STEPS = 2
TOKENS = 1024
TB = 1024
DB = 256
TV = 131072
DV = 32768


def draw_target_logits(key, part):
    key = jax.random.fold_in(key, 11)
    keys = jax.random.split(key, 3)
    cols = jnp.exp(jax.random.uniform(keys[2], (1, TV), minval=math.log(0.7), maxval=math.log(1.4)))
    rows = jnp.exp(jax.random.uniform(keys[1], (TOKENS, 1), minval=math.log(1.5), maxval=math.log(6.0)))
    values = jnp.clip(jax.random.normal(keys[0], (TOKENS, TV)) * rows * cols, -40.0, 40.0)
    return values.astype(jnp.bfloat16)


def draw_draft_hidden(key, part):
    key = jax.random.fold_in(key, 17)
    keys = jax.random.split(key, 2)
    rows = jnp.exp(jax.random.uniform(keys[1], (STEPS, TOKENS, 1), minval=math.log(0.5), maxval=math.log(2.0)))
    values = jnp.clip(jax.random.normal(keys[0], (STEPS, TOKENS, D)), -6.0, 6.0) * rows
    return values.astype(jnp.bfloat16)


def draw_block_map(key, part):
    key = jax.random.fold_in(key, 23)
    keys = jax.random.split(key, 4)
    owners = TB // TBLK_DEV
    total = owners * SEL_MAX
    slots = jnp.arange(total, dtype=jnp.int32)
    owner = slots // SEL_MAX
    heavy = jax.random.randint(keys[0], (), 0, owners)
    noise = jax.random.randint(keys[1], (total,), 0, 4096)
    score = (noise + owner * 4096 // owners) * total + slots
    score = jnp.where(owner == heavy, slots - total, score)
    forced = (slots == 0) | (slots == (owners - 1) * SEL_MAX)
    score = jnp.where(forced, slots - 2 * total, score)
    chosen = jnp.argsort(score, stable=True)[:DB].astype(jnp.int32)
    chosen_owner = chosen // SEL_MAX
    chosen_rank = chosen % SEL_MAX
    owner_ids = jnp.arange(owners, dtype=jnp.int32)[:, None]
    local_ids = jnp.arange(TBLK_DEV, dtype=jnp.int32)[None, :]
    local_scores = jax.random.randint(keys[2], (owners, TBLK_DEV), 0, 1 << 16) * TBLK_DEV + local_ids
    first_low = (owner_ids == 0) & (local_ids == 0)
    last_high = (owner_ids == owners - 1) & (local_ids == TBLK_DEV - 1)
    local_scores = jnp.where(first_low | last_high, -1, local_scores)
    local_order = jnp.argsort(local_scores, axis=1, stable=True).astype(jnp.int32)
    local = local_order[chosen_owner, chosen_rank]
    blocks = chosen_owner * TBLK_DEV + local
    shuffle = jax.random.permutation(keys[3], DB)
    return blocks[shuffle].astype(jnp.int32)


def block_levels(stream_key, shape, pieces, smallest, largest):
    level, own = 1.0, jax.random.fold_in(stream_key, 6)
    for axis_at, shards_of in pieces:
        heights = jnp.exp(jax.random.uniform(jax.random.fold_in(own, axis_at), (shards_of,), jnp.float32, smallest / len(pieces), largest / len(pieces)))
        level = level * jnp.repeat(heights, shape[axis_at] // shards_of).reshape([-1 if axis == axis_at else 1 for axis in range(len(shape))])
    return level


def centred(rng, extent, spread, limit, cuts=(), held_as=jnp.bfloat16):
    array = spread * jax.random.normal(rng, extent, jnp.float32)
    if cuts:
        array = array * block_levels(rng, extent, cuts, -0.22, 0.18)
    return jnp.clip(array, -limit, limit).astype(held_as)


def setup_inputs(seed: int = 0) -> dict:
    arg_keys = jax.random.split(jax.random.key(seed), 5)
    return {
        "target_logits": draw_target_logits(jax.random.fold_in(arg_keys[4], 71), 0),
        "draft_hidden": draw_draft_hidden(jax.random.fold_in(arg_keys[4], 71), 0),
        "draft_head": centred(arg_keys[2], (DV, D), (D // 16) ** -0.5, 0.375, ((0, 64),)),
        "block_map": draw_block_map(jax.random.fold_in(arg_keys[4], 71), 0),
    }


def reference(target_logits, draft_hidden, draft_head, block_map):
    target_vals = target_logits.astype(jnp.float32)
    highest = jnp.max(target_vals, axis=1)
    target_lse = highest + jnp.log(jnp.sum(jnp.exp(target_vals - highest[:, None]), axis=1))
    columns = (block_map[:, None] * BLK + jnp.arange(BLK, dtype=jnp.int32)[None, :]).reshape(-1).astype(jnp.int32)
    picked = jnp.take(target_vals, columns, axis=1)
    target_probs = jnp.exp(picked - target_lse[:, None])
    target_mass = jnp.sum(target_probs, axis=1)
    positions = jnp.arange(TOKENS, dtype=jnp.int32)
    losses = []
    gradients = []
    for step_index in range(STEPS):
        states = draft_hidden[step_index]
        if step_index > 0:
            states = jnp.concatenate([jnp.zeros((step_index, D), jnp.bfloat16), states[:TOKENS - step_index]], axis=0)
        summed = jnp.dot(states, draft_head.T, preferred_element_type=jnp.float32)
        logits = lax.optimization_barrier(summed.astype(jnp.bfloat16)).astype(jnp.float32)
        top_draft = jnp.max(logits, axis=1)
        draft_lse = top_draft + jnp.log(jnp.sum(jnp.exp(logits - top_draft[:, None]), axis=1))
        keep = (positions >= step_index).astype(jnp.float32)
        losses.append(keep * jnp.sum(target_probs * (draft_lse[:, None] - logits), axis=1))
        logit_grads = (64.0 * keep[:, None] * (target_mass[:, None] * jnp.exp(logits - draft_lse[:, None]) - target_probs)).astype(jnp.bfloat16)
        state_grads = jnp.dot(logit_grads, draft_head, preferred_element_type=jnp.float32)
        if step_index > 0:
            state_grads = jnp.concatenate([state_grads[step_index:], jnp.zeros((step_index, D), jnp.float32)], axis=0)
        gradients.append(state_grads)
    return jnp.stack(gradients).astype(jnp.bfloat16), jnp.stack(losses)
```

```python
import jax
import jax.numpy as jnp
from jax import lax
from jax.experimental import pallas as pl
from jax.experimental.pallas import tpu as pltpu
from jax.sharding import PartitionSpec as P

BF = jnp.bfloat16
F32 = jnp.float32
I32 = jnp.int32
MESH = pl.DeviceIdType.MESH
XT_DTYPE = F32

AG1, A2A1, TST, AG2, AGX, A2A2, NBR, STX, STZ, LOS, RSX, RSN, RSS, HEAD = (
    0, 3, 4, 5, 9, 21, 22, 23, 26, 41, 42, 54, 58, 61)
N_SEMS = 62


def nt(a, b):
    return lax.dot_general(a, b, (((1,), (1,)), ((), ())), preferred_element_type=F32)


def mm(a, b):
    return lax.dot_general(a, b, (((1,), (0,)), ((), ())), preferred_element_type=F32)


def onehot(mask):
    return jnp.where(mask, 1.0, 0.0).astype(BF)


def combine(packs):
    t_max = packs[0][0:2]
    k_max = packs[0][4:6]
    d_max = packs[0][8:10]
    for p in packs[1:]:
        t_max = jnp.maximum(t_max, p[0:2])
        k_max = jnp.maximum(k_max, p[4:6])
        d_max = jnp.maximum(d_max, p[8:10])
    t_sum = jnp.zeros((2, 128), F32)
    k_sum = jnp.zeros((2, 128), F32)
    d_sum = jnp.zeros((2, 128), F32)
    term = jnp.zeros((2, 128), F32)
    for p in packs:
        scale = jnp.exp(p[4:6] - k_max)
        t_sum += p[2:4] * jnp.exp(p[0:2] - t_max)
        k_sum += p[6:8] * scale
        d_sum += p[10:12] * jnp.exp(p[8:10] - d_max)
        term += scale * (p[12:14] + p[6:8] * (d_max - p[8:10]))
    return t_max, t_sum, k_max, k_sum, d_max, d_sum, term


def kernel(tl, hid, head_hbm, bmap, grad_out, loss_out,
           head, head_t, xt, send1, recv1, send2, recv2, pick_sel, place, logits,
           tst_send, tst_recv, nbr_send, nbr_recv, stx_send, stx_recv, stz_send, stz_recv,
           los_send, los_recv, wide, own, rsx_send, rsx_recv, rsn_send, rsn_recv, rss_send, rss_recv,
           s_sem, r_sem):
    v = lax.axis_index("vocab")
    t = lax.axis_index("tok")
    z = v // 4
    x = lax.rem(v, 4)
    a = z // 4
    b = lax.rem(z, 4)

    def at_z(off):
        return (lax.rem(z + off + 16, 16) * 4 + x, t)

    def at_x(off):
        return (z * 4 + lax.rem(x + off, 4), t)

    before = (v, lax.rem(t + 7, 8))
    after = (v, lax.rem(t + 1, 8))

    def copy(k, src, dst, dev):
        return pltpu.make_async_remote_copy(
            src_ref=src, dst_ref=dst, send_sem=s_sem.at[k], recv_sem=r_sem.at[k],
            device_id=dev, device_id_type=MESH)

    sent = []

    def send(k, src, dst, dev):
        c = copy(k, src, dst, dev)
        c.start()
        sent.append(c)
        return c

    head_copy = pltpu.make_async_copy(head_hbm, head, r_sem.at[HEAD])
    head_copy.start()

    barrier = pltpu.get_barrier_semaphore()

    def greet(i, c):
        pl.semaphore_signal(barrier, 1, device_id=(lax.rem(v + i, 64), t), device_id_type=MESH)
        return c

    lax.fori_loop(1, 64, greet, 0)
    pl.semaphore_signal(barrier, 1, device_id=before, device_id_type=MESH)
    pl.semaphore_signal(barrier, 1, device_id=after, device_id_type=MESH)

    eye64 = onehot(lax.broadcasted_iota(I32, (64, 64), 0) == lax.broadcasted_iota(I32, (64, 64), 1))
    for s in range(2):
        xt[a, b, x, :, s * 128:(s + 1) * 128] = nt(eye64, hid[s]).astype(BF)

    bm_row = bmap[...]
    own_row = bm_row // 16
    loc_row = (bm_row - own_row * 16).astype(F32)
    own_row = own_row.astype(F32)
    sub = lax.broadcasted_iota(I32, (256, 256), 0)
    lane = lax.broadcasted_iota(I32, (256, 256), 1)
    own_all = jnp.broadcast_to(own_row, (256, 256))
    own_col = jnp.sum(jnp.where(sub == lane, own_all, 0.0), axis=1, keepdims=True)
    rank_row = jnp.sum(jnp.where((own_col == own_all) & (sub < lane), 1.0, 0.0), axis=0, keepdims=True)
    place_row = own_row * 16.0 + rank_row * 2.0
    row16 = lax.broadcasted_iota(I32, (16, 256), 0)
    mine = (jnp.broadcast_to(own_row, (16, 256)) == v.astype(F32)) & (
        jnp.broadcast_to(rank_row, (16, 256)) == (row16 // 2).astype(F32))
    found = jnp.sum(jnp.where(mine, 1.0, 0.0), axis=1, keepdims=True)
    block = jnp.sum(jnp.where(mine, jnp.broadcast_to(loc_row, (16, 256)), 0.0), axis=1, keepdims=True)
    odd = lax.rem(lax.broadcasted_iota(I32, (16, 1), 0), 2)
    first = jnp.where(found > 0.0, block.astype(I32) * 128 + odd, -4096)
    away = lax.broadcasted_iota(I32, (16, 2048), 1) - first

    pl.semaphore_wait(barrier, 65)

    for j in range(1, 4):
        mine_xt = xt.at[a, b, x]
        send(AG1 + j - 1, mine_xt, mine_xt, at_z(4 * j))

    def pick1(g, c):
        sel = jnp.concatenate([onehot(away == 2 * (8 * g + k)) for k in range(8)], axis=0)
        send1[pl.ds(8 * g, 8)] = nt(sel, tl[...]).astype(BF).reshape(8, 16, 128)
        return c

    lax.fori_loop(0, 8, pick1, 0)

    def spread1(i, c):
        p = lax.rem(v + i, 64)
        copy(A2A1, send1.at[p], recv1.at[v], (p, t)).start()
        return c

    lax.fori_loop(1, 64, spread1, 0)
    pltpu.make_async_copy(send1.at[v], recv1.at[v], r_sem.at[A2A1]).start()

    top = tl[:, 0:128].astype(F32)
    for k in range(1, 16):
        top = jnp.maximum(top, tl[:, k * 128:(k + 1) * 128].astype(F32))
    top_col = jnp.max(top, axis=1, keepdims=True)
    total = jnp.zeros((128, 128), F32)
    for k in range(16):
        total += jnp.exp(tl[:, k * 128:(k + 1) * 128].astype(F32) - top_col)
    t_max = jnp.max(top.T, axis=0, keepdims=True)
    t_sum = jnp.sum(total.T, axis=0, keepdims=True)
    tst_send[...] = jnp.concatenate([t_max, t_sum, jnp.zeros((6, 128), F32)], axis=0)
    tst = send(TST, tst_send, tst_recv, before)

    def along_x(o):
        bb = lax.rem(b + o, 4)
        for j in range(1, 4):
            ref = xt.at[:, bb, x]
            send(AGX + 3 * o + j - 1, ref, ref, at_x(j))

    ag1 = [copy(AG1 + j - 1, xt.at[lax.rem(a + 4 - j, 4), b, x], xt.at[lax.rem(a + 4 - j, 4), b, x], at_z(4))
           for j in range(1, 4)]
    for c in ag1:
        c.wait_recv()
    send(AG2, xt.at[:, b, x], xt.at[:, b, x], at_z(1))
    send(AG2 + 1, xt.at[:, b, x], xt.at[:, b, x], at_z(-1))
    send(AG2 + 2, xt.at[pl.ds(0, 2), b, x], xt.at[pl.ds(0, 2), b, x], at_z(-2))
    send(AG2 + 3, xt.at[pl.ds(2, 2), b, x], xt.at[pl.ds(2, 2), b, x], at_z(2))
    along_x(0)

    r512 = lax.broadcasted_iota(I32, (512, 256), 0) // 2
    l512 = lax.broadcasted_iota(I32, (512, 256), 1)
    source = jnp.sum(jnp.where(r512 == l512, jnp.broadcast_to(place_row, (512, 256)), 0.0), axis=1, keepdims=True)
    source = source.astype(I32) + lax.rem(lax.broadcasted_iota(I32, (512, 1), 0), 2)
    pick_sel[...] = onehot(lax.broadcasted_iota(I32, (512, 1024), 1) == source)
    rr = lax.broadcasted_iota(I32, (512, 1), 0)
    goes = (lax.rem(rr, 128) // 2) * 8 + (rr // 128) * 2 + lax.rem(rr, 2)
    place[...] = onehot(lax.broadcasted_iota(I32, (512, 512), 1) == goes)

    def got_x(ref_of, k, dev):
        copy(k, ref_of, ref_of, dev).wait_recv()

    b_prev = lax.rem(b + 3, 4)
    b_next = lax.rem(b + 1, 4)
    b_far = lax.rem(b + 2, 4)
    got_x(xt.at[:, b_prev, x], AG2, at_z(1))
    along_x(3)
    got_x(xt.at[:, b_next, x], AG2 + 1, at_z(1))
    along_x(1)
    got_x(xt.at[pl.ds(0, 2), b_far, x], AG2 + 2, at_z(1))
    got_x(xt.at[pl.ds(2, 2), b_far, x], AG2 + 3, at_z(1))
    along_x(2)

    pltpu.make_async_copy(recv1, recv1, r_sem.at[A2A1]).wait()
    send2[...] = mm(pick_sel[...], recv1[...].reshape(1024, 128)).reshape(64, 8, 128).astype(BF)

    def spread2(i, c):
        p = lax.rem(v + i, 64)
        copy(A2A2, send2.at[p], recv2.at[v], (p, t)).start()
        return c

    lax.fori_loop(1, 64, spread2, 0)
    pltpu.make_async_copy(send2.at[v], recv2.at[v], r_sem.at[A2A2]).start()

    head_copy.wait()
    eye256 = onehot(sub == lane)

    def turn(i, c):
        cols = pl.ds(pl.multiple_of(i * 256, 256), 256)
        head_t[cols, :] = nt(eye256, head[:, cols]).astype(BF)
        return c

    lax.fori_loop(0, 16, turn, 0)

    logits[...] = jnp.zeros((512, 256), F32)
    for o in (0, 3, 1, 2):
        bb = lax.rem(b + o, 4)
        for j in range(1, 4):
            ref = xt.at[:, bb, lax.rem(x + 4 - j, 4)]
            got_x(ref, AGX + 3 * o + j - 1, at_x(1))

        def forward(i, c):
            cols = pl.ds(pl.multiple_of((i * 4 + bb) * 256, 256), 256)
            logits[...] += mm(head[:, cols], xt[i, bb].reshape(256, 256))
            return c

        lax.fori_loop(0, 4, forward, 0)

    pltpu.make_async_copy(recv2, recv2, r_sem.at[A2A2]).wait()
    picked = mm(place[...], recv2[...].reshape(512, 128)).astype(BF)
    r8 = lax.broadcasted_iota(I32, (8, 128), 0)
    l8 = lax.broadcasted_iota(I32, (8, 128), 1)
    nbr_send[...] = nt(onehot((r8 == 0) & (l8 == 0)), picked)
    nbr = send(NBR, nbr_send, nbr_recv, before)
    low = logits[...].astype(BF).astype(F32)
    d_max = jnp.max(low, axis=0, keepdims=True)
    d_sum = jnp.sum(jnp.exp(low - d_max), axis=0, keepdims=True)
    sub128 = lax.broadcasted_iota(I32, (128, 128), 0)
    lane128 = lax.broadcasted_iota(I32, (128, 128), 1)
    nbr.wait_recv()
    moved = mm(picked, onehot(sub128 == lane128 + 1)) + lax.dot_general(
        nbr_recv[...].astype(BF), onehot((r8 == 0) & (l8 == 127)),
        (((0,), (0,)), ((), ())), preferred_element_type=F32)
    picked2 = jnp.concatenate([picked.astype(F32), moved], axis=1)
    k_max = jnp.max(picked2, axis=0, keepdims=True)
    rel = jnp.exp(picked2 - k_max)
    k_sum = jnp.sum(rel, axis=0, keepdims=True)
    term = jnp.sum(rel * (d_max - low), axis=0, keepdims=True)
    tst.wait_recv()
    l1 = lax.broadcasted_iota(I32, (1, 128), 1)

    def moved_row(row, other):
        return jnp.where(l1 == 127, pltpu.roll(other, 127, 1), pltpu.roll(row, 127, 1))

    halves = lambda r: [r[:, 0:128], r[:, 128:256]]
    rows = [t_max, moved_row(t_max, tst_recv[0:1, :]), t_sum, moved_row(t_sum, tst_recv[1:2, :])]
    for r in (k_max, k_sum, d_max, d_sum, term):
        rows += halves(r)
    rows.append(jnp.zeros((2, 128), F32))
    stx_send[...] = jnp.concatenate(rows, axis=0)
    stx = [send(STX + j - 1, stx_send, stx_recv.at[j - 1], at_x(j)) for j in range(1, 4)]
    for c in stx:
        c.wait_recv()
    merged = combine([stx_send[...]] + [stx_recv[j] for j in range(3)])
    stz_send[...] = jnp.concatenate(list(merged) + [jnp.zeros((2, 128), F32)], axis=0)
    stz = [send(STZ + j - 1, stz_send, stz_recv.at[j - 1], at_z(j)) for j in range(1, 16)]
    for c in stz:
        c.wait_recv()
    t_max, t_sum, k_max, k_sum, d_max, d_sum, term = combine(
        [stz_send[...]] + [stz_recv[j] for j in range(15)])
    t_lse = t_max + jnp.log(t_sum)
    lift = jnp.log(d_sum)
    d_lse = d_max + lift
    scale = jnp.exp(k_max - t_lse)
    mass = k_sum * scale
    loss = scale * (term + k_sum * lift)
    los_send[...] = jnp.concatenate([loss, jnp.zeros((6, 128), F32)], axis=0)
    los = send(LOS, los_send, los_recv, after)

    wide_row = lambda r: jnp.concatenate([r[0:1], r[1:2]], axis=1)
    l256 = lax.broadcasted_iota(I32, (1, 256), 1)
    keep = jnp.where((l256 == 255) & (t == 7), 0.0, 64.0)
    low = logits[...].astype(BF).astype(F32)
    grads = (keep * (wide_row(mass) * jnp.exp(low - wide_row(d_lse))
                     - jnp.exp(picked2 - wide_row(t_lse)))).astype(BF)

    for o in (1, 3, 2, 0):
        bb = lax.rem(b + o, 4)

        def backward(i, c):
            cols = pl.ds(pl.multiple_of((i * 4 + bb) * 256, 256), 256)
            part = mm(head_t[cols, :], grads).reshape(4, 64, 256)
            wide[...] = part
            own[o, i] = wide[x]
            for k in range(4):
                rsx_send[o, k, i] = part[k].astype(XT_DTYPE)
            return c

        lax.fori_loop(0, 4, backward, 0)
        for j in range(1, 4):
            send(RSX + 3 * o + j - 1, rsx_send.at[o, lax.rem(x + j, 4)], rsx_recv.at[o, j - 1], at_x(j))

    def summed(o, into):
        for j in range(1, 4):
            ref = rsx_recv.at[o, j - 1]
            copy(RSX + 3 * o + j - 1, ref, ref, at_x(1)).wait_recv()

        def add(i, c):
            into[i] = own[o, i] + rsx_recv[o, 0, i].astype(F32) + rsx_recv[o, 1, i].astype(F32) + rsx_recv[o, 2, i].astype(F32)
            return c

        lax.fori_loop(0, 4, add, 0)

    summed(1, rsn_send.at[0])
    n0 = send(RSN, rsn_send.at[0], rsn_recv.at[0], at_z(1))
    summed(3, rsn_send.at[1])
    n1 = send(RSN + 1, rsn_send.at[1], rsn_recv.at[1], at_z(-1))
    summed(2, rsn_send.at[2])
    n2 = send(RSN + 2, rsn_send.at[2, pl.ds(0, 2)], rsn_recv.at[2, pl.ds(0, 2)], at_z(-2))
    n3 = send(RSN + 3, rsn_send.at[2, pl.ds(2, 2)], rsn_recv.at[2, pl.ds(2, 2)], at_z(2))
    summed(0, rss_send)

    los.wait_recv()
    here = los_send[...]
    other = los_recv[...]
    l8b = lax.broadcasted_iota(I32, (8, 128), 1)
    late = jnp.where(l8b == 0, jnp.where(t == 0, 0.0, pltpu.roll(other, 1, 1)), pltpu.roll(here, 1, 1))
    both = jnp.concatenate([here[0:1], late[1:2]], axis=0)
    l2 = lax.broadcasted_iota(I32, (2, 128), 1)
    for k in range(2):
        loss_out[:, k:k + 1] = jnp.sum(jnp.where(l2 == 2 * v + k, both, 0.0), axis=1, keepdims=True)

    for c in (n0, n1, n2, n3):
        c.wait_recv()

    def add_near(i, c):
        rss_send[i] = rss_send[i] + rsn_recv[0, i] + rsn_recv[1, i] + rsn_recv[2, i]
        return c

    lax.fori_loop(0, 4, add_near, 0)
    far = [send(RSS + j - 1, rss_send.at[lax.rem(a + j, 4)], rss_recv.at[j - 1], at_z(4 * j)) for j in range(1, 4)]
    for c in far:
        c.wait_recv()
    grad = (rss_send[a] + rss_recv[0] + rss_recv[1] + rss_recv[2]).astype(BF)
    eye128 = onehot(sub128 == lane128)
    for s in range(2):
        grad_out[s] = nt(eye128, grad[:, s * 128:(s + 1) * 128]).astype(BF)

    for c in sent:
        c.wait_send()
    for k, ref in ((A2A1, send1), (A2A2, send2)):
        most = ref.at[pl.ds(0, 63)]
        pltpu.make_async_copy(most, most, s_sem.at[k]).wait()


def on_device(target_logits, draft_hidden, draft_head, block_map):
    vm = pl.BlockSpec(memory_space=pltpu.VMEM)
    v = pltpu.VMEM
    return pl.pallas_call(
        kernel,
        name="draft_loss",
        out_shape=(jax.ShapeDtypeStruct((2, 128, 64), BF), jax.ShapeDtypeStruct((2, 2), F32)),
        in_specs=[vm, vm, pl.BlockSpec(memory_space=pl.ANY), vm],
        out_specs=(vm, vm),
        scratch_shapes=[
            v((512, 4096), BF), v((4096, 512), BF), v((4, 4, 4, 64, 256), BF),
            v((64, 16, 128), BF), v((64, 16, 128), BF), v((64, 8, 128), BF), v((64, 8, 128), BF),
            v((512, 1024), BF), v((512, 512), BF), v((512, 256), F32),
            v((8, 128), F32), v((8, 128), F32), v((8, 512), F32), v((8, 512), F32),
            v((16, 128), F32), v((3, 16, 128), F32), v((16, 128), F32), v((15, 16, 128), F32),
            v((8, 128), F32), v((8, 128), F32),
            v((4, 64, 256), F32), v((4, 4, 64, 256), F32),
            v((4, 4, 4, 64, 256), XT_DTYPE), v((4, 3, 4, 64, 256), XT_DTYPE),
            v((3, 4, 64, 256), F32), v((3, 4, 64, 256), F32),
            v((4, 64, 256), F32), v((3, 64, 256), F32),
            pltpu.SemaphoreType.DMA((N_SEMS,)), pltpu.SemaphoreType.DMA((N_SEMS,)),
        ],
        compiler_params=pltpu.CompilerParams(
            collective_id=0, has_side_effects=True, vmem_limit_bytes=50 * 1024 * 1024),
        cost_estimate=pl.CostEstimate(flops=2 ** 31, bytes_accessed=5 * 2 ** 20, transcendentals=2 ** 20),
    )(target_logits, draft_hidden, draft_head, block_map.reshape(1, 256))


def solution(mesh):
    return jax.shard_map(
        on_device,
        mesh=mesh,
        in_specs=(P("tok", "vocab"), P(None, "tok", "vocab"), P("vocab", None), P()),
        out_specs=(P(None, "tok", "vocab"), P(None, ("tok", "vocab"))),
        check_vma=False,
    )
```

```python
import jax
import jax.numpy as jnp
from jax import lax
from jax.experimental import pallas as pl
from jax.experimental.pallas import tpu as pltpu
from jax.sharding import PartitionSpec as P

BF = jnp.bfloat16
F32 = jnp.float32
I32 = jnp.int32
MESH = pl.DeviceIdType.MESH
XT_DTYPE = BF

COUNTS = dict(AG1=3, A2A1=1, LSX=3, LSZ=15, LSN=1, AG2=4, AGX=12, A2A2=1, NBR=1, STX=3, STZ=15, LOS=1,
              RSX=24, RSN=8, RSS=6, HEAD=1, TL=1, HID=2, MAP=1)
BASE = {}
N_SEMS = 0
for _name, _count in COUNTS.items():
    BASE[_name] = N_SEMS
    N_SEMS += _count
AG1, A2A1, LSX, LSZ, LSN, AG2, AGX, A2A2, NBR, STX, STZ, LOS, RSX, RSN, RSS, HEAD, TL, HID, MAP = BASE.values()


def nt(a, b):
    return lax.dot_general(a, b, (((1,), (1,)), ((), ())), preferred_element_type=F32)


def mm(a, b):
    return lax.dot_general(a, b, (((1,), (0,)), ((), ())), preferred_element_type=F32)


def onehot(mask):
    return jnp.where(mask, 1.0, 0.0).astype(BF)


def combine_lse(packs):
    top = packs[0][0:1]
    for p in packs[1:]:
        top = jnp.maximum(top, p[0:1])
    total = jnp.zeros((1, 128), F32)
    for p in packs:
        total += p[1:2] * jnp.exp(p[0:1] - top)
    return jnp.concatenate([top, total, jnp.zeros((6, 128), F32)], axis=0)


def combine(packs):
    top = packs[0][0:2]
    for p in packs[1:]:
        top = jnp.maximum(top, p[0:2])
    total = jnp.zeros((2, 128), F32)
    mass = jnp.zeros((2, 128), F32)
    term = jnp.zeros((2, 128), F32)
    for p in packs:
        rise = top - p[0:2]
        total += p[2:4] * jnp.exp(-rise)
        mass += p[4:6]
        term += p[6:8] + p[4:6] * rise
    return top, total, mass, term


def kernel(tl_hbm, hid_hbm, head_hbm, bmap_hbm, grad_out, loss_out,
           bmap, tl, head, head_t, xt, send1, recv1, send2, recv2, pick_sel, place, logits, probs,
           lsx_send, lsx_recv, lsz_send, lsz_recv, lse_send, lse_recv, nbr_send, nbr_recv,
           stx_send, stx_recv, stz_send, stz_recv, los_send, los_recv, wide, own,
           rsx_send, rsx_recv, rsn_send, rsn_recv, rss_send, rss_recv, s_sem, r_sem):
    v = lax.axis_index("vocab")
    t = lax.axis_index("tok")
    z = v // 4
    x = lax.rem(v, 4)
    a = z // 4
    b = lax.rem(z, 4)

    def at_z(off):
        return (lax.rem(z + off + 16, 16) * 4 + x, t)

    def at_x(off):
        return (z * 4 + lax.rem(x + off, 4), t)

    before = (v, lax.rem(t + 7, 8))
    after = (v, lax.rem(t + 1, 8))

    def copy(k, src, dst, dev):
        return pltpu.make_async_remote_copy(
            src_ref=src, dst_ref=dst, send_sem=s_sem.at[k], recv_sem=r_sem.at[k],
            device_id=dev, device_id_type=MESH)

    sent = []

    def send(k, src, dst, dev):
        c = copy(k, src, dst, dev)
        c.start()
        sent.append(c)
        return c

    hid_copies = [pltpu.make_async_copy(hid_hbm.at[s], xt.at[a, b, x, :, pl.ds(s * 128, 128)], r_sem.at[HID + s])
                  for s in range(2)]
    for c in hid_copies:
        c.start()
    map_copy = pltpu.make_async_copy(bmap_hbm, bmap, r_sem.at[MAP])
    map_copy.start()
    tl_copy = pltpu.make_async_copy(tl_hbm, tl, r_sem.at[TL])
    tl_copy.start()
    head_copy = pltpu.make_async_copy(head_hbm, head, r_sem.at[HEAD])
    head_copy.start()

    barrier = pltpu.get_barrier_semaphore()

    def greet(i, c):
        pl.semaphore_signal(barrier, 1, device_id=(lax.rem(v + i, 64), t), device_id_type=MESH)
        return c

    lax.fori_loop(1, 64, greet, 0)
    pl.semaphore_signal(barrier, 1, device_id=before, device_id_type=MESH)
    pl.semaphore_signal(barrier, 1, device_id=after, device_id_type=MESH)

    map_copy.wait()
    bm_row = bmap[...]
    own_row = bm_row // 16
    loc_row = (bm_row - own_row * 16).astype(F32)
    own_row = own_row.astype(F32)
    sub = lax.broadcasted_iota(I32, (256, 256), 0)
    lane = lax.broadcasted_iota(I32, (256, 256), 1)
    own_all = jnp.broadcast_to(own_row, (256, 256))
    own_col = jnp.sum(jnp.where(sub == lane, own_all, 0.0), axis=1, keepdims=True)
    rank_row = jnp.sum(jnp.where((own_col == own_all) & (sub < lane), 1.0, 0.0), axis=0, keepdims=True)
    place_row = own_row * 16.0 + rank_row * 2.0
    row16 = lax.broadcasted_iota(I32, (16, 256), 0)
    mine = (jnp.broadcast_to(own_row, (16, 256)) == v.astype(F32)) & (
        jnp.broadcast_to(rank_row, (16, 256)) == (row16 // 2).astype(F32))
    found = jnp.sum(jnp.where(mine, 1.0, 0.0), axis=1, keepdims=True)
    block = jnp.sum(jnp.where(mine, jnp.broadcast_to(loc_row, (16, 256)), 0.0), axis=1, keepdims=True)
    odd = lax.rem(lax.broadcasted_iota(I32, (16, 1), 0), 2)
    first = jnp.where(found > 0.0, block.astype(I32) * 128 + odd, -4096)
    away = lax.broadcasted_iota(I32, (16, 2048), 1) - first

    for c in hid_copies:
        c.wait()
    pl.semaphore_wait(barrier, 65)

    for j in range(1, 4):
        mine_xt = xt.at[a, b, x]
        send(AG1 + j - 1, mine_xt, mine_xt, at_z(4 * j))

    tl_copy.wait()

    def pick1(g, c):
        sel = jnp.concatenate([onehot(away == 2 * (8 * g + k)) for k in range(8)], axis=0)
        send1[pl.ds(8 * g, 8)] = nt(sel, tl[...]).astype(BF).reshape(8, 16, 128)
        return c

    lax.fori_loop(0, 8, pick1, 0)

    def spread1(i, c):
        p = lax.rem(v + i, 64)
        copy(A2A1, send1.at[p], recv1.at[v], (p, t)).start()
        return c

    lax.fori_loop(1, 64, spread1, 0)
    pltpu.make_async_copy(send1.at[v], recv1.at[v], r_sem.at[A2A1]).start()

    top = tl[:, 0:128].astype(F32)
    for k in range(1, 16):
        top = jnp.maximum(top, tl[:, k * 128:(k + 1) * 128].astype(F32))
    top_col = jnp.max(top, axis=1, keepdims=True)
    total = jnp.zeros((128, 128), F32)
    for k in range(16):
        total += jnp.exp(tl[:, k * 128:(k + 1) * 128].astype(F32) - top_col)
    t_max = jnp.max(top.T, axis=0, keepdims=True)
    t_sum = jnp.sum(total.T, axis=0, keepdims=True)
    lsx_send[...] = jnp.concatenate([t_max, t_sum, jnp.zeros((6, 128), F32)], axis=0)
    lsx = [send(LSX + j - 1, lsx_send, lsx_recv.at[j - 1], at_x(j)) for j in range(1, 4)]

    def along_x(o):
        bb = lax.rem(b + o, 4)
        for j in range(1, 4):
            ref = xt.at[:, bb, x]
            send(AGX + 3 * o + j - 1, ref, ref, at_x(j))

    ag1 = [copy(AG1 + j - 1, xt.at[lax.rem(a + 4 - j, 4), b, x], xt.at[lax.rem(a + 4 - j, 4), b, x], at_z(4))
           for j in range(1, 4)]
    for c in ag1:
        c.wait_recv()
    send(AG2, xt.at[:, b, x], xt.at[:, b, x], at_z(1))
    send(AG2 + 1, xt.at[:, b, x], xt.at[:, b, x], at_z(-1))
    send(AG2 + 2, xt.at[pl.ds(0, 2), b, x], xt.at[pl.ds(0, 2), b, x], at_z(-2))
    send(AG2 + 3, xt.at[pl.ds(2, 2), b, x], xt.at[pl.ds(2, 2), b, x], at_z(2))
    along_x(0)

    for c in lsx:
        c.wait_recv()
    lsz_send[...] = combine_lse([lsx_send[...]] + [lsx_recv[j] for j in range(3)])
    lsz = [send(LSZ + j - 1, lsz_send, lsz_recv.at[j - 1], at_z(j)) for j in range(1, 16)]

    r512 = lax.broadcasted_iota(I32, (512, 256), 0) // 2
    l512 = lax.broadcasted_iota(I32, (512, 256), 1)
    source = jnp.sum(jnp.where(r512 == l512, jnp.broadcast_to(place_row, (512, 256)), 0.0), axis=1, keepdims=True)
    source = source.astype(I32) + lax.rem(lax.broadcasted_iota(I32, (512, 1), 0), 2)
    pick_sel[...] = onehot(lax.broadcasted_iota(I32, (512, 1024), 1) == source)
    rr = lax.broadcasted_iota(I32, (512, 1), 0)
    goes = (lax.rem(rr, 128) // 2) * 8 + (rr // 128) * 2 + lax.rem(rr, 2)
    place[...] = onehot(lax.broadcasted_iota(I32, (512, 512), 1) == goes)

    def got_x(ref_of, k, dev):
        copy(k, ref_of, ref_of, dev).wait_recv()

    b_prev = lax.rem(b + 3, 4)
    b_next = lax.rem(b + 1, 4)
    b_far = lax.rem(b + 2, 4)
    got_x(xt.at[:, b_prev, x], AG2, at_z(1))
    along_x(3)
    got_x(xt.at[:, b_next, x], AG2 + 1, at_z(1))
    along_x(1)
    got_x(xt.at[pl.ds(0, 2), b_far, x], AG2 + 2, at_z(1))
    got_x(xt.at[pl.ds(2, 2), b_far, x], AG2 + 3, at_z(1))
    along_x(2)

    pltpu.make_async_copy(recv1, recv1, r_sem.at[A2A1]).wait()
    send2[...] = mm(pick_sel[...], recv1[...].reshape(1024, 128)).reshape(64, 8, 128).astype(BF)

    def spread2(i, c):
        p = lax.rem(v + i, 64)
        copy(A2A2, send2.at[p], recv2.at[v], (p, t)).start()
        return c

    lax.fori_loop(1, 64, spread2, 0)
    pltpu.make_async_copy(send2.at[v], recv2.at[v], r_sem.at[A2A2]).start()

    head_copy.wait()
    eye256 = onehot(sub == lane)

    def turn(i, c):
        cols = pl.ds(pl.multiple_of(i * 256, 256), 256)
        head_t[cols, :] = nt(eye256, head[:, cols]).astype(BF)
        return c

    lax.fori_loop(0, 16, turn, 0)

    logits[...] = jnp.zeros((512, 256), F32)
    for o in (0, 3, 1, 2):
        bb = lax.rem(b + o, 4)
        for j in range(1, 4):
            ref = xt.at[:, bb, lax.rem(x + 4 - j, 4)]
            got_x(ref, AGX + 3 * o + j - 1, at_x(1))

        def forward(i, c):
            cols = pl.ds(pl.multiple_of((i * 4 + bb) * 256, 256), 256)
            logits[...] += mm(head[:, cols], xt[i, bb].reshape(256, 256))
            return c

        lax.fori_loop(0, 4, forward, 0)

    for c in lsz:
        c.wait_recv()
    stat = combine_lse([lsz_send[...]] + [lsz_recv[j] for j in range(15)])
    lse_send[...] = jnp.broadcast_to(stat[0:1] + jnp.log(stat[1:2]), (8, 128))
    lse_copy = send(LSN, lse_send, lse_recv, before)

    pltpu.make_async_copy(recv2, recv2, r_sem.at[A2A2]).wait()
    picked = mm(place[...], recv2[...].reshape(512, 128)).astype(BF)
    r8 = lax.broadcasted_iota(I32, (8, 128), 0)
    l8 = lax.broadcasted_iota(I32, (8, 128), 1)
    nbr_send[...] = nt(onehot((r8 == 0) & (l8 == 0)), picked)
    nbr = send(NBR, nbr_send, nbr_recv, before)
    low = logits[...].astype(BF).astype(F32)
    d_max = jnp.max(low, axis=0, keepdims=True)
    d_sum = jnp.sum(jnp.exp(low - d_max), axis=0, keepdims=True)
    sub128 = lax.broadcasted_iota(I32, (128, 128), 0)
    lane128 = lax.broadcasted_iota(I32, (128, 128), 1)
    nbr.wait_recv()
    moved = mm(picked, onehot(sub128 == lane128 + 1)) + lax.dot_general(
        nbr_recv[...].astype(BF), onehot((r8 == 0) & (l8 == 127)),
        (((0,), (0,)), ((), ())), preferred_element_type=F32)
    picked2 = jnp.concatenate([picked.astype(F32), moved], axis=1)
    lse_copy.wait_recv()
    l1 = lax.broadcasted_iota(I32, (1, 128), 1)
    t_lse = lse_send[0:1, :]
    moved_lse = jnp.where(l1 == 127, pltpu.roll(lse_recv[0:1, :], 127, 1), pltpu.roll(t_lse, 127, 1))
    probs[...] = jnp.exp(picked2 - jnp.concatenate([t_lse, moved_lse], axis=1))
    mass = jnp.sum(probs[...], axis=0, keepdims=True)
    term = jnp.sum(probs[...] * (d_max - low), axis=0, keepdims=True)
    rows = []
    for r in (d_max, d_sum, mass, term):
        rows += [r[:, 0:128], r[:, 128:256]]
    stx_send[...] = jnp.concatenate(rows, axis=0)
    stx = [send(STX + j - 1, stx_send, stx_recv.at[j - 1], at_x(j)) for j in range(1, 4)]
    for c in stx:
        c.wait_recv()
    stz_send[...] = jnp.concatenate(combine([stx_send[...]] + [stx_recv[j] for j in range(3)]), axis=0)
    stz = [send(STZ + j - 1, stz_send, stz_recv.at[j - 1], at_z(j)) for j in range(1, 16)]
    for c in stz:
        c.wait_recv()
    d_max, d_sum, mass, term = combine([stz_send[...]] + [stz_recv[j] for j in range(15)])
    lift = jnp.log(d_sum)
    d_lse = d_max + lift
    loss = term + mass * lift
    los_send[...] = jnp.concatenate([loss, jnp.zeros((6, 128), F32)], axis=0)
    los = send(LOS, los_send, los_recv, after)

    wide_row = lambda r: jnp.concatenate([r[0:1], r[1:2]], axis=1)
    l256 = lax.broadcasted_iota(I32, (1, 256), 1)
    keep = jnp.where((l256 == 255) & (t == 7), 0.0, 64.0)
    low = logits[...].astype(BF).astype(F32)
    grads = (keep * (wide_row(mass) * jnp.exp(low - wide_row(d_lse))
                     - probs[...])).astype(BF)

    def along_x_back(s, o):
        for j in range(1, 4):
            send(RSX + 12 * s + 3 * o + j - 1, rsx_send.at[s, o, lax.rem(x + j, 4)], rsx_recv.at[s, o, j - 1], at_x(j))

    for o in (1, 3, 2, 0):
        bb = lax.rem(b + o, 4)

        def backward(i, c):
            cols = pl.ds(pl.multiple_of((i * 4 + bb) * 256, 256), 256)
            part = mm(head_t[cols, :], grads).reshape(4, 64, 256)
            wide[...] = part
            for s in range(2):
                half = slice(s * 128, (s + 1) * 128)
                own[s, o, i] = wide[x, :, half]
                for k in range(4):
                    rsx_send[s, o, k, i] = part[k, :, half].astype(XT_DTYPE)
            return c

        lax.fori_loop(0, 4, backward, 0)
        along_x_back(0, o)
    for o in (1, 3, 2, 0):
        along_x_back(1, o)

    def summed(s, o, into):
        for j in range(1, 4):
            ref = rsx_recv.at[s, o, j - 1]
            copy(RSX + 12 * s + 3 * o + j - 1, ref, ref, at_x(1)).wait_recv()

        def add(i, c):
            into[i] = own[s, o, i] + rsx_recv[s, o, 0, i].astype(F32) + rsx_recv[s, o, 1, i].astype(F32) + rsx_recv[s, o, 2, i].astype(F32)
            return c

        lax.fori_loop(0, 4, add, 0)

    near = {0: [], 1: []}

    def to_near(s, o):
        k = RSN + 4 * s
        if o == 1:
            summed(s, o, rsn_send.at[s, 0])
            near[s].append(send(k, rsn_send.at[s, 0], rsn_recv.at[s, 0], at_z(1)))
        elif o == 3:
            summed(s, o, rsn_send.at[s, 1])
            near[s].append(send(k + 1, rsn_send.at[s, 1], rsn_recv.at[s, 1], at_z(-1)))
        else:
            summed(s, o, rsn_send.at[s, 2])
            low2, high2 = pl.ds(0, 2), pl.ds(2, 2)
            near[s].append(send(k + 2, rsn_send.at[s, 2, low2], rsn_recv.at[s, 2, low2], at_z(-2)))
            near[s].append(send(k + 3, rsn_send.at[s, 2, high2], rsn_recv.at[s, 2, high2], at_z(2)))

    def to_far(s):
        for c in near[s]:
            c.wait_recv()

        def add_near(i, c):
            rss_send[s, i] = rss_send[s, i] + rsn_recv[s, 0, i] + rsn_recv[s, 1, i] + rsn_recv[s, 2, i]
            return c

        lax.fori_loop(0, 4, add_near, 0)
        return [send(RSS + 3 * s + j - 1, rss_send.at[s, lax.rem(a + j, 4)], rss_recv.at[s, j - 1], at_z(4 * j))
                for j in range(1, 4)]

    for o in (1, 3, 2):
        to_near(0, o)
    summed(0, 0, rss_send.at[0])
    to_near(1, 1)
    far = to_far(0)
    to_near(1, 3)
    to_near(1, 2)
    summed(1, 0, rss_send.at[1])
    far += to_far(1)

    los.wait_recv()
    here = los_send[...]
    other = los_recv[...]
    l8b = lax.broadcasted_iota(I32, (8, 128), 1)
    late = jnp.where(l8b == 0, jnp.where(t == 0, 0.0, pltpu.roll(other, 1, 1)), pltpu.roll(here, 1, 1))
    both = jnp.concatenate([here[0:1], late[1:2]], axis=0)
    l2 = lax.broadcasted_iota(I32, (2, 128), 1)
    for k in range(2):
        loss_out[:, k:k + 1] = jnp.sum(jnp.where(l2 == 2 * v + k, both, 0.0), axis=1, keepdims=True)

    for c in far:
        c.wait_recv()
    for s in range(2):
        grad_out[s] = (rss_send[s, a] + rss_recv[s, 0] + rss_recv[s, 1] + rss_recv[s, 2]).astype(BF)

    for c in sent:
        c.wait_send()
    for k, ref in ((A2A1, send1), (A2A2, send2)):
        most = ref.at[pl.ds(0, 63)]
        pltpu.make_async_copy(most, most, s_sem.at[k]).wait()


def on_device(target_logits, draft_hidden, draft_head, block_map):
    vm = pl.BlockSpec(memory_space=pltpu.VMEM)
    hbm = pl.BlockSpec(memory_space=pltpu.HBM)
    v = pltpu.VMEM
    tile = v((8, 128), F32)
    grad, loss = pl.pallas_call(
        kernel,
        name="draft_loss",
        out_shape=(jax.ShapeDtypeStruct((2, 64, 128), BF), jax.ShapeDtypeStruct((2, 2), F32)),
        in_specs=[hbm, hbm, hbm, hbm],
        out_specs=(vm, vm),
        scratch_shapes=[
            v((1, 256), I32), v((128, 2048), BF), v((512, 4096), BF), v((4096, 512), BF), v((4, 4, 4, 64, 256), BF),
            v((64, 16, 128), BF), v((64, 16, 128), BF), v((64, 8, 128), BF), v((64, 8, 128), BF),
            v((512, 1024), BF), v((512, 512), BF), v((512, 256), F32), v((512, 256), F32),
            tile, v((3, 8, 128), F32), tile, v((15, 8, 128), F32), tile, tile, v((8, 512), F32), v((8, 512), F32),
            tile, v((3, 8, 128), F32), tile, v((15, 8, 128), F32), tile, tile,
            v((4, 64, 256), F32), v((2, 4, 4, 64, 128), F32),
            v((2, 4, 4, 4, 64, 128), XT_DTYPE), v((2, 4, 3, 4, 64, 128), XT_DTYPE),
            v((2, 3, 4, 64, 128), F32), v((2, 3, 4, 64, 128), F32),
            v((2, 4, 64, 128), F32), v((2, 3, 64, 128), F32),
            pltpu.SemaphoreType.DMA((N_SEMS,)), pltpu.SemaphoreType.DMA((N_SEMS,)),
        ],
        compiler_params=pltpu.CompilerParams(
            collective_id=0, has_side_effects=True, vmem_limit_bytes=62 * 1024 * 1024),
        cost_estimate=pl.CostEstimate(flops=2 ** 31, bytes_accessed=5 * 2 ** 20, transcendentals=2 ** 20),
    )(target_logits, draft_hidden.transpose(0, 2, 1), draft_head, block_map.reshape(1, 256))
    return grad.transpose(0, 2, 1), loss


def solution(mesh):
    return jax.shard_map(
        on_device,
        mesh=mesh,
        in_specs=(P("tok", "vocab"), P(None, "tok", "vocab"), P("vocab", None), P()),
        out_specs=(P(None, "tok", "vocab"), P(None, ("tok", "vocab"))),
        check_vma=False,
    )
```

```python
import jax
import jax.numpy as jnp
from jax import lax
from jax.experimental import pallas as pl
from jax.experimental.pallas import tpu as pltpu
from jax.sharding import PartitionSpec as P

BF = jnp.bfloat16
F32 = jnp.float32
I32 = jnp.int32
MESH = pl.DeviceIdType.MESH
XT_DTYPE = BF

COUNTS = dict(AG1=3, A2A1=1, LSX=3, LSZ=15, LSN=1, AG2=4, AGX=12, A2A2=1, NBR=1, STX=3, STZ=15, LOX=3, LOZ=15, LOS=1,
              RSX=24, RSN=8, RSS=6, HEAD=1, TL=1, HID=2, MAP=1)
BASE = {}
N_SEMS = 0
for _name, _count in COUNTS.items():
    BASE[_name] = N_SEMS
    N_SEMS += _count
AG1, A2A1, LSX, LSZ, LSN, AG2, AGX, A2A2, NBR, STX, STZ, LOX, LOZ, LOS, RSX, RSN, RSS, HEAD, TL, HID, MAP = BASE.values()


def nt(a, b):
    return lax.dot_general(a, b, (((1,), (1,)), ((), ())), preferred_element_type=F32)


def mm(a, b):
    return lax.dot_general(a, b, (((1,), (0,)), ((), ())), preferred_element_type=F32)


def onehot(mask):
    return jnp.where(mask, 1.0, 0.0).astype(BF)


def combine_target(packs):
    top = packs[0][0:1]
    for p in packs[1:]:
        top = jnp.maximum(top, p[0:1])
    sums = jnp.zeros((2, 128), F32)
    for p in packs:
        sums += p[1:3] * jnp.exp(p[0:1] - top)
    return jnp.concatenate([top, sums, jnp.zeros((5, 128), F32)], axis=0)


def combine(packs):
    top = packs[0][0:2]
    for p in packs[1:]:
        top = jnp.maximum(top, p[0:2])
    total = jnp.zeros((2, 128), F32)
    for p in packs:
        total += p[2:4] * jnp.exp(p[0:2] - top)
    return jnp.concatenate([top, total], axis=0)


def kernel(tl_hbm, hid_hbm, head_hbm, bmap_hbm, grad_out, loss_out,
           bmap, tl, head, head_t, xt, send1, recv1, send2, recv2, pick_sel, place, logits, probs,
           lsx_send, lsx_recv, lsz_send, lsz_recv, lse_send, lse_recv, nbr_send, nbr_recv,
           stx_send, stx_recv, stz_send, stz_recv,
           lox_send, lox_recv, loz_send, loz_recv, los_send, los_recv, wide, own,
           rsx_send, rsx_recv, rsn_send, rsn_recv, rss_send, rss_recv, s_sem, r_sem):
    v = lax.axis_index("vocab")
    t = lax.axis_index("tok")
    z = v // 4
    x = lax.rem(v, 4)
    a = z // 4
    b = lax.rem(z, 4)

    def at_z(off):
        return (lax.rem(z + off + 16, 16) * 4 + x, t)

    def at_x(off):
        return (z * 4 + lax.rem(x + off, 4), t)

    before = (v, lax.rem(t + 7, 8))
    after = (v, lax.rem(t + 1, 8))

    def copy(k, src, dst, dev):
        return pltpu.make_async_remote_copy(
            src_ref=src, dst_ref=dst, send_sem=s_sem.at[k], recv_sem=r_sem.at[k],
            device_id=dev, device_id_type=MESH)

    sent = []

    def send(k, src, dst, dev):
        c = copy(k, src, dst, dev)
        c.start()
        sent.append(c)
        return c

    hid_copies = [pltpu.make_async_copy(hid_hbm.at[s], xt.at[a, b, x, :, pl.ds(s * 128, 128)], r_sem.at[HID + s])
                  for s in range(2)]
    for c in hid_copies:
        c.start()
    map_copy = pltpu.make_async_copy(bmap_hbm, bmap, r_sem.at[MAP])
    map_copy.start()
    tl_copy = pltpu.make_async_copy(tl_hbm, tl, r_sem.at[TL])
    tl_copy.start()
    head_copy = pltpu.make_async_copy(head_hbm, head, r_sem.at[HEAD])
    head_copy.start()

    barrier = pltpu.get_barrier_semaphore()

    def greet(i, c):
        pl.semaphore_signal(barrier, 1, device_id=(lax.rem(v + i, 64), t), device_id_type=MESH)
        return c

    lax.fori_loop(1, 64, greet, 0)
    pl.semaphore_signal(barrier, 1, device_id=before, device_id_type=MESH)
    pl.semaphore_signal(barrier, 1, device_id=after, device_id_type=MESH)

    map_copy.wait()
    bm_row = bmap[...]
    own_row = bm_row // 16
    loc_row = (bm_row - own_row * 16).astype(F32)
    own_row = own_row.astype(F32)
    sub = lax.broadcasted_iota(I32, (256, 256), 0)
    lane = lax.broadcasted_iota(I32, (256, 256), 1)
    own_all = jnp.broadcast_to(own_row, (256, 256))
    own_col = jnp.sum(jnp.where(sub == lane, own_all, 0.0), axis=1, keepdims=True)
    rank_row = jnp.sum(jnp.where((own_col == own_all) & (sub < lane), 1.0, 0.0), axis=0, keepdims=True)
    place_row = own_row * 16.0 + rank_row * 2.0
    row16 = lax.broadcasted_iota(I32, (16, 256), 0)
    mine = (jnp.broadcast_to(own_row, (16, 256)) == v.astype(F32)) & (
        jnp.broadcast_to(rank_row, (16, 256)) == (row16 // 2).astype(F32))
    found = jnp.sum(jnp.where(mine, 1.0, 0.0), axis=1, keepdims=True)
    block = jnp.sum(jnp.where(mine, jnp.broadcast_to(loc_row, (16, 256)), 0.0), axis=1, keepdims=True)
    odd = lax.rem(lax.broadcasted_iota(I32, (16, 1), 0), 2)
    mapped = jnp.max(jnp.where((jnp.broadcast_to(own_row, (16, 256)) == v.astype(F32)) & (
        jnp.broadcast_to(loc_row, (16, 256)) == row16.astype(F32)), 1.0, 0.0), axis=1, keepdims=True)
    first = jnp.where(found > 0.0, block.astype(I32) * 128 + odd, -4096)
    away = lax.broadcasted_iota(I32, (16, 2048), 1) - first

    for c in hid_copies:
        c.wait()
    pl.semaphore_wait(barrier, 65)

    for j in range(1, 4):
        mine_xt = xt.at[a, b, x]
        send(AG1 + j - 1, mine_xt, mine_xt, at_z(4 * j))

    tl_copy.wait()

    top = tl[:, 0:128].astype(F32)
    for k in range(1, 16):
        top = jnp.maximum(top, tl[:, k * 128:(k + 1) * 128].astype(F32))
    top_col = jnp.max(top, axis=1, keepdims=True)
    total = jnp.zeros((128, 128), F32)
    kept = jnp.zeros((128, 128), F32)
    for k in range(16):
        weight = jnp.exp(tl[:, k * 128:(k + 1) * 128].astype(F32) - top_col)
        total += weight
        kept += weight * mapped[k:k + 1, :]
    t_max = jnp.max(top.T, axis=0, keepdims=True)
    t_sum = jnp.sum(total.T, axis=0, keepdims=True)
    t_kept = jnp.sum(kept.T, axis=0, keepdims=True)
    lsx_send[...] = jnp.concatenate([t_max, t_sum, t_kept, jnp.zeros((5, 128), F32)], axis=0)
    lsx = [send(LSX + j - 1, lsx_send, lsx_recv.at[j - 1], at_x(j)) for j in range(1, 4)]

    def pick1(g, c):
        sel = jnp.concatenate([onehot(away == 2 * (8 * g + k)) for k in range(8)], axis=0)
        send1[pl.ds(8 * g, 8)] = nt(sel, tl[...]).astype(BF).reshape(8, 16, 128)
        return c

    lax.fori_loop(0, 8, pick1, 0)

    def along_x(o):
        bb = lax.rem(b + o, 4)
        for j in range(1, 4):
            ref = xt.at[:, bb, x]
            send(AGX + 3 * o + j - 1, ref, ref, at_x(j))

    ag1 = [copy(AG1 + j - 1, xt.at[lax.rem(a + 4 - j, 4), b, x], xt.at[lax.rem(a + 4 - j, 4), b, x], at_z(4))
           for j in range(1, 4)]
    for c in ag1:
        c.wait_recv()
    send(AG2, xt.at[:, b, x], xt.at[:, b, x], at_z(1))
    send(AG2 + 1, xt.at[:, b, x], xt.at[:, b, x], at_z(-1))
    send(AG2 + 2, xt.at[pl.ds(0, 2), b, x], xt.at[pl.ds(0, 2), b, x], at_z(-2))
    send(AG2 + 3, xt.at[pl.ds(2, 2), b, x], xt.at[pl.ds(2, 2), b, x], at_z(2))
    along_x(0)

    def spread1(i, c):
        p = lax.rem(v + i, 64)
        copy(A2A1, send1.at[p], recv1.at[v], (p, t)).start()
        return c

    lax.fori_loop(1, 64, spread1, 0)
    pltpu.make_async_copy(send1.at[v], recv1.at[v], r_sem.at[A2A1]).start()

    for c in lsx:
        c.wait_recv()
    lsz_send[...] = combine_target([lsx_send[...]] + [lsx_recv[j] for j in range(3)])
    lsz = [send(LSZ + j - 1, lsz_send, lsz_recv.at[j - 1], at_z(j)) for j in range(1, 16)]

    r512 = lax.broadcasted_iota(I32, (512, 256), 0) // 2
    l512 = lax.broadcasted_iota(I32, (512, 256), 1)
    source = jnp.sum(jnp.where(r512 == l512, jnp.broadcast_to(place_row, (512, 256)), 0.0), axis=1, keepdims=True)
    source = source.astype(I32) + lax.rem(lax.broadcasted_iota(I32, (512, 1), 0), 2)
    pick_sel[...] = onehot(lax.broadcasted_iota(I32, (512, 1024), 1) == source)
    rr = lax.broadcasted_iota(I32, (512, 1), 0)
    goes = (lax.rem(rr, 128) // 2) * 8 + (rr // 128) * 2 + lax.rem(rr, 2)
    place[...] = onehot(lax.broadcasted_iota(I32, (512, 512), 1) == goes)

    def got_x(ref_of, k, dev):
        copy(k, ref_of, ref_of, dev).wait_recv()

    b_prev = lax.rem(b + 3, 4)
    b_next = lax.rem(b + 1, 4)
    b_far = lax.rem(b + 2, 4)
    got_x(xt.at[:, b_prev, x], AG2, at_z(1))
    along_x(3)
    got_x(xt.at[:, b_next, x], AG2 + 1, at_z(1))
    along_x(1)
    got_x(xt.at[pl.ds(0, 2), b_far, x], AG2 + 2, at_z(1))
    got_x(xt.at[pl.ds(2, 2), b_far, x], AG2 + 3, at_z(1))
    along_x(2)

    head_copy.wait()
    eye256 = onehot(sub == lane)

    def turn(i, c):
        cols = pl.ds(pl.multiple_of(i * 256, 256), 256)
        head_t[cols, :] = nt(eye256, head[:, cols]).astype(BF)
        return c

    lax.fori_loop(0, 16, turn, 0)

    for c in lsz:
        c.wait_recv()
    stat = combine_target([lsz_send[...]] + [lsz_recv[j] for j in range(15)])
    t_lse = stat[0:1] + jnp.log(stat[1:2])
    t_mass = stat[2:3] * jnp.exp(stat[0:1] - t_lse)
    lse_send[...] = jnp.concatenate([t_lse, t_mass, jnp.zeros((6, 128), F32)], axis=0)
    lse_copy = send(LSN, lse_send, lse_recv, before)

    def exchange_again():
        pltpu.make_async_copy(recv1, recv1, r_sem.at[A2A1]).wait()
        send2[...] = mm(pick_sel[...], recv1[...].reshape(1024, 128)).reshape(64, 8, 128).astype(BF)

        def spread2(i, c):
            p = lax.rem(v + i, 64)
            copy(A2A2, send2.at[p], recv2.at[v], (p, t)).start()
            return c

        lax.fori_loop(1, 64, spread2, 0)
        pltpu.make_async_copy(send2.at[v], recv2.at[v], r_sem.at[A2A2]).start()

    logits[...] = jnp.zeros((512, 256), F32)
    for o in (0, 3, 1, 2):
        if o == 2:
            exchange_again()
        bb = lax.rem(b + o, 4)
        for j in range(1, 4):
            ref = xt.at[:, bb, lax.rem(x + 4 - j, 4)]
            got_x(ref, AGX + 3 * o + j - 1, at_x(1))

        def forward(i, c):
            cols = pl.ds(pl.multiple_of((i * 4 + bb) * 256, 256), 256)
            logits[...] += mm(head[:, cols], xt[i, bb].reshape(256, 256))
            return c

        lax.fori_loop(0, 4, forward, 0)

    low = logits[...].astype(BF).astype(F32)
    d_max = jnp.max(low, axis=0, keepdims=True)
    d_sum = jnp.sum(jnp.exp(low - d_max), axis=0, keepdims=True)
    stx_send[...] = jnp.concatenate([d_max[:, 0:128], d_max[:, 128:], d_sum[:, 0:128], d_sum[:, 128:]], axis=0)
    stx = [send(STX + j - 1, stx_send, stx_recv.at[j - 1], at_x(j)) for j in range(1, 4)]
    lse_copy.wait_recv()
    l1 = lax.broadcasted_iota(I32, (1, 128), 1)

    def with_next(k):
        row = lse_send[k:k + 1, :]
        late = jnp.where(l1 == 127, pltpu.roll(lse_recv[k:k + 1, :], 127, 1), pltpu.roll(row, 127, 1))
        return jnp.concatenate([row, late], axis=1)

    t_lse = with_next(0)
    mass = with_next(1)
    for c in stx:
        c.wait_recv()
    stz_send[...] = combine([stx_send[...]] + [stx_recv[j] for j in range(3)])
    stz = [send(STZ + j - 1, stz_send, stz_recv.at[j - 1], at_z(j)) for j in range(1, 16)]

    pltpu.make_async_copy(recv2, recv2, r_sem.at[A2A2]).wait()
    picked = mm(place[...], recv2[...].reshape(512, 128)).astype(BF)
    r8 = lax.broadcasted_iota(I32, (8, 128), 0)
    l8 = lax.broadcasted_iota(I32, (8, 128), 1)
    nbr_send[...] = nt(onehot((r8 == 0) & (l8 == 0)), picked)
    nbr = send(NBR, nbr_send, nbr_recv, before)
    sub128 = lax.broadcasted_iota(I32, (128, 128), 0)
    lane128 = lax.broadcasted_iota(I32, (128, 128), 1)
    moved = mm(picked, onehot(sub128 == lane128 + 1))
    nbr.wait_recv()
    moved += lax.dot_general(
        nbr_recv[...].astype(BF), onehot((r8 == 0) & (l8 == 127)),
        (((0,), (0,)), ((), ())), preferred_element_type=F32)
    probs[...] = jnp.exp(jnp.concatenate([picked.astype(F32), moved], axis=1) - t_lse)

    for c in stz:
        c.wait_recv()
    stat = combine([stz_send[...]] + [stz_recv[j] for j in range(15)])
    d_lse = stat[0:2] + jnp.log(stat[2:4])

    d_lse = jnp.concatenate([d_lse[0:1], d_lse[1:2]], axis=1)
    l256 = lax.broadcasted_iota(I32, (1, 256), 1)
    keep = jnp.where((l256 == 255) & (t == 7), 0.0, 64.0)
    low = logits[...].astype(BF).astype(F32)
    grads = (keep * (mass * jnp.exp(low - d_lse) - probs[...])).astype(BF)

    def along_x_back(s, o):
        for j in range(1, 4):
            send(RSX + 12 * s + 3 * o + j - 1, rsx_send.at[s, o, lax.rem(x + j, 4)], rsx_recv.at[s, o, j - 1], at_x(j))

    for o in (1, 3, 2, 0):
        bb = lax.rem(b + o, 4)

        def backward(i, c):
            cols = pl.ds(pl.multiple_of((i * 4 + bb) * 256, 256), 256)
            part = mm(head_t[cols, :], grads).reshape(4, 64, 256)
            wide[...] = part
            for s in range(2):
                half = slice(s * 128, (s + 1) * 128)
                own[s, o, i] = wide[x, :, half]
                for k in range(4):
                    rsx_send[s, o, k, i] = part[k, :, half].astype(XT_DTYPE)
            return c

        lax.fori_loop(0, 4, backward, 0)
        along_x_back(0, o)
    for o in (1, 3, 2, 0):
        along_x_back(1, o)

    loss = jnp.sum(probs[...] * (d_lse - logits[...].astype(BF).astype(F32)), axis=0, keepdims=True)
    lox_send[...] = jnp.concatenate([loss[:, 0:128], loss[:, 128:]], axis=0)
    lox = [send(LOX + j - 1, lox_send, lox_recv.at[j - 1], at_x(j)) for j in range(1, 4)]

    def loss_on():
        for c in lox:
            c.wait_recv()
        loz_send[...] = lox_send[...] + lox_recv[0] + lox_recv[1] + lox_recv[2]
        return [send(LOZ + j - 1, loz_send, loz_recv.at[j - 1], at_z(j)) for j in range(1, 16)]

    def loss_over(loz):
        for c in loz:
            c.wait_recv()
        whole = loz_send[...]
        for j in range(15):
            whole += loz_recv[j]
        los_send[...] = jnp.concatenate([whole, jnp.zeros((6, 128), F32)], axis=0)
        return send(LOS, los_send, los_recv, after)

    def summed(s, o, into):
        for j in range(1, 4):
            ref = rsx_recv.at[s, o, j - 1]
            copy(RSX + 12 * s + 3 * o + j - 1, ref, ref, at_x(1)).wait_recv()

        def add(i, c):
            into[i] = own[s, o, i] + rsx_recv[s, o, 0, i].astype(F32) + rsx_recv[s, o, 1, i].astype(F32) + rsx_recv[s, o, 2, i].astype(F32)
            return c

        lax.fori_loop(0, 4, add, 0)

    near = {0: [], 1: []}

    def to_near(s, o):
        k = RSN + 4 * s
        if o == 1:
            summed(s, o, rsn_send.at[s, 0])
            near[s].append(send(k, rsn_send.at[s, 0], rsn_recv.at[s, 0], at_z(1)))
        elif o == 3:
            summed(s, o, rsn_send.at[s, 1])
            near[s].append(send(k + 1, rsn_send.at[s, 1], rsn_recv.at[s, 1], at_z(-1)))
        else:
            summed(s, o, rsn_send.at[s, 2])
            low2, high2 = pl.ds(0, 2), pl.ds(2, 2)
            near[s].append(send(k + 2, rsn_send.at[s, 2, low2], rsn_recv.at[s, 2, low2], at_z(-2)))
            near[s].append(send(k + 3, rsn_send.at[s, 2, high2], rsn_recv.at[s, 2, high2], at_z(2)))

    def to_far(s):
        for c in near[s]:
            c.wait_recv()

        def add_near(i, c):
            rss_send[s, i] = rss_send[s, i] + rsn_recv[s, 0, i] + rsn_recv[s, 1, i] + rsn_recv[s, 2, i]
            return c

        lax.fori_loop(0, 4, add_near, 0)
        return [send(RSS + 3 * s + j - 1, rss_send.at[s, lax.rem(a + j, 4)], rss_recv.at[s, j - 1], at_z(4 * j))
                for j in range(1, 4)]

    to_near(0, 1)
    to_near(0, 3)
    loz = loss_on()
    to_near(0, 2)
    summed(0, 0, rss_send.at[0])
    to_near(1, 1)
    far = to_far(0)
    to_near(1, 3)
    los = loss_over(loz)
    to_near(1, 2)
    summed(1, 0, rss_send.at[1])
    far += to_far(1)

    los.wait_recv()
    here = los_send[...]
    other = los_recv[...]
    l8b = lax.broadcasted_iota(I32, (8, 128), 1)
    late = jnp.where(l8b == 0, jnp.where(t == 0, 0.0, pltpu.roll(other, 1, 1)), pltpu.roll(here, 1, 1))
    both = jnp.concatenate([here[0:1], late[1:2]], axis=0)
    l2 = lax.broadcasted_iota(I32, (2, 128), 1)
    for k in range(2):
        loss_out[:, k:k + 1] = jnp.sum(jnp.where(l2 == 2 * v + k, both, 0.0), axis=1, keepdims=True)

    for c in far:
        c.wait_recv()
    for s in range(2):
        grad_out[s] = (rss_send[s, a] + rss_recv[s, 0] + rss_recv[s, 1] + rss_recv[s, 2]).astype(BF)

    for c in sent:
        c.wait_send()
    for k, ref in ((A2A1, send1), (A2A2, send2)):
        most = ref.at[pl.ds(0, 63)]
        pltpu.make_async_copy(most, most, s_sem.at[k]).wait()


def on_device(target_logits, draft_hidden, draft_head, block_map):
    vm = pl.BlockSpec(memory_space=pltpu.VMEM)
    hbm = pl.BlockSpec(memory_space=pltpu.HBM)
    v = pltpu.VMEM
    tile = v((8, 128), F32)
    grad, loss = pl.pallas_call(
        kernel,
        name="draft_loss",
        out_shape=(jax.ShapeDtypeStruct((2, 64, 128), BF), jax.ShapeDtypeStruct((2, 2), F32)),
        in_specs=[hbm, hbm, hbm, hbm],
        out_specs=(vm, vm),
        scratch_shapes=[
            v((1, 256), I32), v((128, 2048), BF), v((512, 4096), BF), v((4096, 512), BF), v((4, 4, 4, 64, 256), BF),
            v((64, 16, 128), BF), v((64, 16, 128), BF), v((64, 8, 128), BF), v((64, 8, 128), BF),
            v((512, 1024), BF), v((512, 512), BF), v((512, 256), F32), v((512, 256), F32),
            tile, v((3, 8, 128), F32), tile, v((15, 8, 128), F32), tile, tile, v((8, 512), F32), v((8, 512), F32),
            v((4, 128), F32), v((3, 4, 128), F32), v((4, 128), F32), v((15, 4, 128), F32),
            v((2, 128), F32), v((3, 2, 128), F32), v((2, 128), F32), v((15, 2, 128), F32), tile, tile,
            v((4, 64, 256), F32), v((2, 4, 4, 64, 128), F32),
            v((2, 4, 4, 4, 64, 128), XT_DTYPE), v((2, 4, 3, 4, 64, 128), XT_DTYPE),
            v((2, 3, 4, 64, 128), F32), v((2, 3, 4, 64, 128), F32),
            v((2, 4, 64, 128), F32), v((2, 3, 64, 128), F32),
            pltpu.SemaphoreType.DMA((N_SEMS,)), pltpu.SemaphoreType.DMA((N_SEMS,)),
        ],
        compiler_params=pltpu.CompilerParams(
            collective_id=0, has_side_effects=True, vmem_limit_bytes=62 * 1024 * 1024),
        cost_estimate=pl.CostEstimate(flops=2 ** 31, bytes_accessed=5 * 2 ** 20, transcendentals=2 ** 20),
    )(target_logits, draft_hidden.transpose(0, 2, 1), draft_head, block_map.reshape(1, 256))
    return grad.transpose(0, 2, 1), loss


def solution(mesh):
    return jax.shard_map(
        on_device,
        mesh=mesh,
        in_specs=(P("tok", "vocab"), P(None, "tok", "vocab"), P("vocab", None), P()),
        out_specs=(P(None, "tok", "vocab"), P(None, ("tok", "vocab"))),
        check_vma=False,
    )
```

```python
import jax
import jax.numpy as jnp
from jax import lax
from jax.experimental import pallas as pl
from jax.experimental.pallas import tpu as pltpu
from jax.sharding import PartitionSpec as P

BF = jnp.bfloat16
F32 = jnp.float32
I32 = jnp.int32
MESH = pl.DeviceIdType.MESH

COUNTS = dict(AG1=3, A2A1=1, LSX=3, LSZ=15, LSN=1, AG2=4, AGX=12, A2A2=1, NBR=1, STX=3, STZ=15, LOX=3, LOZ=15, LOS=1,
              RSX=12, RSN=4, RSZ=4, RSY=3, RSS=6, HEAD=1, TL=1, HID=2, MAP=1)
BASE = {}
N_SEMS = 0
for _name, _count in COUNTS.items():
    BASE[_name] = N_SEMS
    N_SEMS += _count
AG1, A2A1, LSX, LSZ, LSN, AG2, AGX, A2A2, NBR, STX, STZ, LOX, LOZ, LOS, RSX, RSN, RSZ, RSY, RSS, HEAD, TL, HID, MAP = BASE.values()


def nt(a, b):
    return lax.dot_general(a, b, (((1,), (1,)), ((), ())), preferred_element_type=F32)


def mm(a, b):
    return lax.dot_general(a, b, (((1,), (0,)), ((), ())), preferred_element_type=F32)


def onehot(mask):
    return jnp.where(mask, 1.0, 0.0).astype(BF)


def combine_target(packs):
    top = packs[0][0:1]
    for p in packs[1:]:
        top = jnp.maximum(top, p[0:1])
    sums = jnp.zeros((2, 128), F32)
    for p in packs:
        sums += p[1:3] * jnp.exp(p[0:1] - top)
    return jnp.concatenate([top, sums, jnp.zeros((5, 128), F32)], axis=0)


def combine(packs):
    top = packs[0][0:2]
    for p in packs[1:]:
        top = jnp.maximum(top, p[0:2])
    total = jnp.zeros((2, 128), F32)
    for p in packs:
        total += p[2:4] * jnp.exp(p[0:2] - top)
    return jnp.concatenate([top, total], axis=0)


def kernel(tl_hbm, hid_hbm, head_hbm, bmap_hbm, grad_out, loss_out,
           bmap, tl, head, head_t, xt, send1, recv1, send2, recv2, pick_sel, place, logits, probs,
           lsx_send, lsx_recv, lsz_send, lsz_recv, lse_send, lse_recv, nbr_send, nbr_recv,
           stx_send, stx_recv, stz_send, stz_recv,
           lox_send, lox_recv, loz_send, loz_recv, los_send, los_recv, wide, own, own_z,
           rsx_send, rsx_recv, rsn_send, rsn_recv, rsz_send, rsz_recv, rsy_recv, rss_send, rss_recv, s_sem, r_sem):
    v = lax.axis_index("vocab")
    t = lax.axis_index("tok")
    z = v // 4
    x = lax.rem(v, 4)
    a = z // 4
    b = lax.rem(z, 4)

    def at_z(off):
        return (lax.rem(z + off + 16, 16) * 4 + x, t)

    def at_x(off):
        return (z * 4 + lax.rem(x + off, 4), t)

    before = (v, lax.rem(t + 7, 8))
    after = (v, lax.rem(t + 1, 8))

    def copy(k, src, dst, dev):
        return pltpu.make_async_remote_copy(
            src_ref=src, dst_ref=dst, send_sem=s_sem.at[k], recv_sem=r_sem.at[k],
            device_id=dev, device_id_type=MESH)

    sent = []

    def send(k, src, dst, dev):
        c = copy(k, src, dst, dev)
        c.start()
        sent.append(c)
        return c

    hid_copies = [pltpu.make_async_copy(hid_hbm.at[s], xt.at[a, b, x, :, pl.ds(s * 128, 128)], r_sem.at[HID + s])
                  for s in range(2)]
    for c in hid_copies:
        c.start()
    map_copy = pltpu.make_async_copy(bmap_hbm, bmap, r_sem.at[MAP])
    map_copy.start()
    tl_copy = pltpu.make_async_copy(tl_hbm, tl, r_sem.at[TL])
    tl_copy.start()
    head_copy = pltpu.make_async_copy(head_hbm, head, r_sem.at[HEAD])
    head_copy.start()

    barrier = pltpu.get_barrier_semaphore()

    def greet(i, c):
        pl.semaphore_signal(barrier, 1, device_id=(lax.rem(v + i, 64), t), device_id_type=MESH)
        return c

    lax.fori_loop(1, 64, greet, 0)
    pl.semaphore_signal(barrier, 1, device_id=before, device_id_type=MESH)
    pl.semaphore_signal(barrier, 1, device_id=after, device_id_type=MESH)

    map_copy.wait()
    bm_row = bmap[...]
    own_row = bm_row // 16
    loc_row = (bm_row - own_row * 16).astype(F32)
    own_row = own_row.astype(F32)
    sub = lax.broadcasted_iota(I32, (256, 256), 0)
    lane = lax.broadcasted_iota(I32, (256, 256), 1)
    own_all = jnp.broadcast_to(own_row, (256, 256))
    own_col = jnp.sum(jnp.where(sub == lane, own_all, 0.0), axis=1, keepdims=True)
    rank_row = jnp.sum(jnp.where((own_col == own_all) & (sub < lane), 1.0, 0.0), axis=0, keepdims=True)
    place_row = own_row * 16.0 + rank_row * 2.0
    row16 = lax.broadcasted_iota(I32, (16, 256), 0)
    mine = (jnp.broadcast_to(own_row, (16, 256)) == v.astype(F32)) & (
        jnp.broadcast_to(rank_row, (16, 256)) == (row16 // 2).astype(F32))
    found = jnp.sum(jnp.where(mine, 1.0, 0.0), axis=1, keepdims=True)
    block = jnp.sum(jnp.where(mine, jnp.broadcast_to(loc_row, (16, 256)), 0.0), axis=1, keepdims=True)
    odd = lax.rem(lax.broadcasted_iota(I32, (16, 1), 0), 2)
    mapped = jnp.max(jnp.where((jnp.broadcast_to(own_row, (16, 256)) == v.astype(F32)) & (
        jnp.broadcast_to(loc_row, (16, 256)) == row16.astype(F32)), 1.0, 0.0), axis=1, keepdims=True)
    first = jnp.where(found > 0.0, block.astype(I32) * 128 + odd, -4096)
    away = lax.broadcasted_iota(I32, (16, 2048), 1) - first

    for c in hid_copies:
        c.wait()
    pl.semaphore_wait(barrier, 65)

    for j in range(1, 4):
        mine_xt = xt.at[a, b, x]
        send(AG1 + j - 1, mine_xt, mine_xt, at_z(4 * j))

    tl_copy.wait()

    def targets():
        top = tl[:, 0:128].astype(F32)
        for k in range(1, 16):
            top = jnp.maximum(top, tl[:, k * 128:(k + 1) * 128].astype(F32))
        top_col = jnp.max(top, axis=1, keepdims=True)
        total = jnp.zeros((128, 128), F32)
        kept = jnp.zeros((128, 128), F32)
        for k in range(16):
            weight = jnp.exp(tl[:, k * 128:(k + 1) * 128].astype(F32) - top_col)
            total += weight
            kept += weight * mapped[k:k + 1, :]
        t_max = jnp.max(top.T, axis=0, keepdims=True)
        t_sum = jnp.sum(total.T, axis=0, keepdims=True)
        t_kept = jnp.sum(kept.T, axis=0, keepdims=True)
        lsx_send[...] = jnp.concatenate([t_max, t_sum, t_kept, jnp.zeros((5, 128), F32)], axis=0)
        return [send(LSX + j - 1, lsx_send, lsx_recv.at[j - 1], at_x(j)) for j in range(1, 4)]

    def picks():
        def pick1(g, c):
            sel = jnp.concatenate([onehot(away == 2 * (8 * g + k)) for k in range(8)], axis=0)
            send1[pl.ds(8 * g, 8)] = nt(sel, tl[...]).astype(BF).reshape(8, 16, 128)
            return c

        lax.fori_loop(0, 8, pick1, 0)

    def spread():
        def spread1(i, c):
            p = lax.rem(v + i, 64)
            copy(A2A1, send1.at[p], recv1.at[v], (p, t)).start()
            return c

        lax.fori_loop(1, 64, spread1, 0)
        pltpu.make_async_copy(send1.at[v], recv1.at[v], r_sem.at[A2A1]).start()

    lsx = targets()
    picks()

    def along_x(o):
        bb = lax.rem(b + o, 4)
        for j in range(1, 4):
            ref = xt.at[:, bb, x]
            send(AGX + 3 * o + j - 1, ref, ref, at_x(j))

    ag1 = [copy(AG1 + j - 1, xt.at[lax.rem(a + 4 - j, 4), b, x], xt.at[lax.rem(a + 4 - j, 4), b, x], at_z(4))
           for j in range(1, 4)]
    for c in ag1:
        c.wait_recv()
    send(AG2, xt.at[:, b, x], xt.at[:, b, x], at_z(1))
    send(AG2 + 1, xt.at[:, b, x], xt.at[:, b, x], at_z(-1))
    send(AG2 + 2, xt.at[pl.ds(0, 2), b, x], xt.at[pl.ds(0, 2), b, x], at_z(-2))
    send(AG2 + 3, xt.at[pl.ds(2, 2), b, x], xt.at[pl.ds(2, 2), b, x], at_z(2))
    along_x(0)

    for c in lsx:
        c.wait_recv()
    lsz_send[...] = combine_target([lsx_send[...]] + [lsx_recv[j] for j in range(3)])
    lsz = [send(LSZ + j - 1, lsz_send, lsz_recv.at[j - 1], at_z(j)) for j in range(1, 16)]

    r512 = lax.broadcasted_iota(I32, (512, 256), 0) // 2
    l512 = lax.broadcasted_iota(I32, (512, 256), 1)
    source = jnp.sum(jnp.where(r512 == l512, jnp.broadcast_to(place_row, (512, 256)), 0.0), axis=1, keepdims=True)
    source = source.astype(I32) + lax.rem(lax.broadcasted_iota(I32, (512, 1), 0), 2)
    pick_sel[...] = onehot(lax.broadcasted_iota(I32, (512, 1024), 1) == source)
    rr = lax.broadcasted_iota(I32, (512, 1), 0)
    goes = (lax.rem(rr, 128) // 2) * 8 + (rr // 128) * 2 + lax.rem(rr, 2)
    place[...] = onehot(lax.broadcasted_iota(I32, (512, 512), 1) == goes)

    def got_x(ref_of, k, dev):
        copy(k, ref_of, ref_of, dev).wait_recv()

    b_prev = lax.rem(b + 3, 4)
    b_next = lax.rem(b + 1, 4)
    b_far = lax.rem(b + 2, 4)
    got_x(xt.at[:, b_prev, x], AG2, at_z(1))
    along_x(3)
    got_x(xt.at[:, b_next, x], AG2 + 1, at_z(1))
    along_x(1)
    got_x(xt.at[pl.ds(0, 2), b_far, x], AG2 + 2, at_z(1))
    got_x(xt.at[pl.ds(2, 2), b_far, x], AG2 + 3, at_z(1))
    along_x(2)
    spread()

    def exchange_again():
        pltpu.make_async_copy(recv1, recv1, r_sem.at[A2A1]).wait()
        send2[...] = mm(pick_sel[...], recv1[...].reshape(1024, 128)).reshape(64, 8, 128).astype(BF)

        def spread2(i, c):
            p = lax.rem(v + i, 64)
            copy(A2A2, send2.at[p], recv2.at[v], (p, t)).start()
            return c

        lax.fori_loop(1, 64, spread2, 0)
        pltpu.make_async_copy(send2.at[v], recv2.at[v], r_sem.at[A2A2]).start()

    head_copy.wait()
    eye256 = onehot(sub == lane)

    def turn(i, c):
        cols = pl.ds(pl.multiple_of(i * 256, 256), 256)
        head_t[cols, :] = nt(eye256, head[:, cols]).astype(BF)
        return c

    lax.fori_loop(0, 16, turn, 0)

    for c in lsz:
        c.wait_recv()
    stat = combine_target([lsz_send[...]] + [lsz_recv[j] for j in range(15)])
    t_lse = stat[0:1] + jnp.log(stat[1:2])
    t_mass = stat[2:3] * jnp.exp(stat[0:1] - t_lse)
    lse_send[...] = jnp.concatenate([t_lse, t_mass, jnp.zeros((6, 128), F32)], axis=0)
    lse_copy = send(LSN, lse_send, lse_recv, before)

    logits[...] = jnp.zeros((512, 256), F32)
    for o in (0, 3, 1, 2):
        if o == 2:
            exchange_again()
        bb = lax.rem(b + o, 4)
        for j in range(1, 4):
            ref = xt.at[:, bb, lax.rem(x + 4 - j, 4)]
            got_x(ref, AGX + 3 * o + j - 1, at_x(1))

        def forward(i, c):
            cols = pl.ds(pl.multiple_of((i * 4 + bb) * 256, 256), 256)
            logits[...] += mm(head[:, cols], xt[i, bb].reshape(256, 256))
            return c

        lax.fori_loop(0, 4, forward, 0)

    low = logits[...].astype(BF).astype(F32)
    d_max = jnp.max(low, axis=0, keepdims=True)
    d_sum = jnp.sum(jnp.exp(low - d_max), axis=0, keepdims=True)
    stx_send[...] = jnp.concatenate([d_max[:, 0:128], d_max[:, 128:], d_sum[:, 0:128], d_sum[:, 128:]], axis=0)
    stx = [send(STX + j - 1, stx_send, stx_recv.at[j - 1], at_x(j)) for j in range(1, 4)]
    lse_copy.wait_recv()
    l1 = lax.broadcasted_iota(I32, (1, 128), 1)

    def with_next(k):
        row = lse_send[k:k + 1, :]
        late = jnp.where(l1 == 127, pltpu.roll(lse_recv[k:k + 1, :], 127, 1), pltpu.roll(row, 127, 1))
        return jnp.concatenate([row, late], axis=1)

    t_lse = with_next(0)
    mass = with_next(1)
    for c in stx:
        c.wait_recv()
    stz_send[...] = combine([stx_send[...]] + [stx_recv[j] for j in range(3)])
    stz = [send(STZ + j - 1, stz_send, stz_recv.at[j - 1], at_z(j)) for j in range(1, 16)]

    pltpu.make_async_copy(recv2, recv2, r_sem.at[A2A2]).wait()
    picked = mm(place[...], recv2[...].reshape(512, 128)).astype(BF)
    r8 = lax.broadcasted_iota(I32, (8, 128), 0)
    l8 = lax.broadcasted_iota(I32, (8, 128), 1)
    nbr_send[...] = nt(onehot((r8 == 0) & (l8 == 0)), picked)
    nbr = send(NBR, nbr_send, nbr_recv, before)
    sub128 = lax.broadcasted_iota(I32, (128, 128), 0)
    lane128 = lax.broadcasted_iota(I32, (128, 128), 1)
    moved = mm(picked, onehot(sub128 == lane128 + 1))
    nbr.wait_recv()
    moved += lax.dot_general(
        nbr_recv[...].astype(BF), onehot((r8 == 0) & (l8 == 127)),
        (((0,), (0,)), ((), ())), preferred_element_type=F32)
    probs[...] = jnp.exp(jnp.concatenate([picked.astype(F32), moved], axis=1) - t_lse)

    for c in stz:
        c.wait_recv()
    stat = combine([stz_send[...]] + [stz_recv[j] for j in range(15)])
    d_lse = stat[0:2] + jnp.log(stat[2:4])

    d_lse = jnp.concatenate([d_lse[0:1], d_lse[1:2]], axis=1)
    l256 = lax.broadcasted_iota(I32, (1, 256), 1)
    keep = jnp.where((l256 == 255) & (t == 7), 0.0, 64.0)
    low = logits[...].astype(BF).astype(F32)
    grads = (keep * (mass * jnp.exp(low - d_lse) - probs[...])).astype(BF)

    loss = jnp.sum(probs[...] * (d_lse - logits[...].astype(BF).astype(F32)), axis=0, keepdims=True)
    lox_send[...] = jnp.concatenate([loss[:, 0:128], loss[:, 128:]], axis=0)
    lox = [send(LOX + j - 1, lox_send, lox_recv.at[j - 1], at_x(j)) for j in range(1, 4)]

    def along_x_back(o):
        for j in range(1, 4):
            send(RSX + 3 * o + j - 1, rsx_send.at[o, lax.rem(x + j, 4)], rsx_recv.at[o, j - 1], at_x(j))

    first_z = []
    for o in (1, 3, 2, 0):
        bb = lax.rem(b + o, 4)

        def backward(i, c):
            cols = pl.ds(pl.multiple_of((i * 4 + bb) * 256, 256), 256)
            part = mm(head_t[cols, :], grads).reshape(4, 64, 256)
            wide[...] = part
            own[o, i] = wide[x, :, 0:128]
            for k in range(4):
                rsx_send[o, k, i] = part[k, :, 0:128].astype(BF)
                if o == 0:
                    own_z[k, i] = part[k, :, 128:256]
                else:
                    rsz_send[o - 1, k, i] = part[k, :, 128:256].astype(BF)
            return c

        lax.fori_loop(0, 4, backward, 0)
        along_x_back(o)
        if o == 1:
            first_z.append(send(RSZ, rsz_send.at[0], rsz_recv.at[0], at_z(1)))
        elif o == 3:
            first_z.append(send(RSZ + 1, rsz_send.at[2], rsz_recv.at[2], at_z(-1)))
        elif o == 2:
            for k, part in ((0, pl.ds(0, 2)), (1, pl.ds(2, 2))):
                first_z.append(send(RSZ + 2 + k, rsz_send.at[1, :, part], rsz_recv.at[1, :, part], at_z(4 * k - 2)))

    def loss_on():
        for c in lox:
            c.wait_recv()
        loz_send[...] = lox_send[...] + lox_recv[0] + lox_recv[1] + lox_recv[2]
        return [send(LOZ + j - 1, loz_send, loz_recv.at[j - 1], at_z(j)) for j in range(1, 16)]

    def loss_over(loz):
        for c in loz:
            c.wait_recv()
        whole = loz_send[...]
        for j in range(15):
            whole += loz_recv[j]
        los_send[...] = jnp.concatenate([whole, jnp.zeros((6, 128), F32)], axis=0)
        return send(LOS, los_send, los_recv, after)

    def summed(o, into):
        for j in range(1, 4):
            ref = rsx_recv.at[o, j - 1]
            copy(RSX + 3 * o + j - 1, ref, ref, at_x(1)).wait_recv()

        def add(i, c):
            into[i] = own[o, i] + rsx_recv[o, 0, i].astype(F32) + rsx_recv[o, 1, i].astype(F32) + rsx_recv[o, 2, i].astype(F32)
            return c

        lax.fori_loop(0, 4, add, 0)

    def to_far(s, first, parts):
        def add_last(i, c):
            rss_send[s, i] = first(i) + parts[0, i] + parts[1, i] + parts[2, i]
            return c

        lax.fori_loop(0, 4, add_last, 0)
        return [send(RSS + 3 * s + j - 1, rss_send.at[s, lax.rem(a + j, 4)], rss_recv.at[s, j - 1], at_z(4 * j))
                for j in range(1, 4)]

    loz = loss_on()
    near = []
    for o in (1, 3, 2):
        summed(o, rsn_send.at[o - 1])
        if o == 1:
            near.append(send(RSN, rsn_send.at[0], rsn_recv.at[0], at_z(1)))
        elif o == 3:
            near.append(send(RSN + 1, rsn_send.at[2], rsn_recv.at[2], at_z(-1)))
        else:
            for k, part in ((0, pl.ds(0, 2)), (1, pl.ds(2, 2))):
                near.append(send(RSN + 2 + k, rsn_send.at[1, part], rsn_recv.at[1, part], at_z(4 * k - 2)))
    for c in first_z:
        c.wait_recv()

    def add_z(i, c):
        for k in range(4):
            own_z[k, i] = (own_z[k, i] + rsz_recv[0, k, i].astype(F32) + rsz_recv[1, k, i].astype(F32)
                           + rsz_recv[2, k, i].astype(F32))
        return c

    lax.fori_loop(0, 4, add_z, 0)
    then_x = [send(RSY + j - 1, own_z.at[lax.rem(x + j, 4)], rsy_recv.at[j - 1], at_x(j)) for j in range(1, 4)]
    summed(0, rss_send.at[0])
    for c in near:
        c.wait_recv()
    far = to_far(0, lambda i: rss_send[0, i], rsn_recv)
    los = loss_over(loz)
    for c in then_x:
        c.wait_recv()
    far += to_far(1, lambda i: own_z[x, i], rsy_recv)

    los.wait_recv()
    here = los_send[...]
    other = los_recv[...]
    l8b = lax.broadcasted_iota(I32, (8, 128), 1)
    late = jnp.where(l8b == 0, jnp.where(t == 0, 0.0, pltpu.roll(other, 1, 1)), pltpu.roll(here, 1, 1))
    both = jnp.concatenate([here[0:1], late[1:2]], axis=0)
    l2 = lax.broadcasted_iota(I32, (2, 128), 1)
    for k in range(2):
        loss_out[:, k:k + 1] = jnp.sum(jnp.where(l2 == 2 * v + k, both, 0.0), axis=1, keepdims=True)

    for c in far:
        c.wait_recv()
    for s in range(2):
        grad_out[s] = (rss_send[s, a] + rss_recv[s, 0] + rss_recv[s, 1] + rss_recv[s, 2]).astype(BF)

    for c in sent:
        c.wait_send()
    for k, ref in ((A2A1, send1), (A2A2, send2)):
        most = ref.at[pl.ds(0, 63)]
        pltpu.make_async_copy(most, most, s_sem.at[k]).wait()


def on_device(target_logits, draft_hidden, draft_head, block_map):
    vm = pl.BlockSpec(memory_space=pltpu.VMEM)
    hbm = pl.BlockSpec(memory_space=pltpu.HBM)
    v = pltpu.VMEM
    tile = v((8, 128), F32)
    grad, loss = pl.pallas_call(
        kernel,
        name="draft_loss",
        out_shape=(jax.ShapeDtypeStruct((2, 64, 128), BF), jax.ShapeDtypeStruct((2, 2), F32)),
        in_specs=[hbm, hbm, hbm, hbm],
        out_specs=(vm, vm),
        scratch_shapes=[
            v((1, 256), I32), v((128, 2048), BF), v((512, 4096), BF), v((4096, 512), BF), v((4, 4, 4, 64, 256), BF),
            v((64, 16, 128), BF), v((64, 16, 128), BF), v((64, 8, 128), BF), v((64, 8, 128), BF),
            v((512, 1024), BF), v((512, 512), BF), v((512, 256), F32), v((512, 256), F32),
            tile, v((3, 8, 128), F32), tile, v((15, 8, 128), F32), tile, tile, v((8, 512), F32), v((8, 512), F32),
            v((4, 128), F32), v((3, 4, 128), F32), v((4, 128), F32), v((15, 4, 128), F32),
            v((2, 128), F32), v((3, 2, 128), F32), v((2, 128), F32), v((15, 2, 128), F32), tile, tile,
            v((4, 64, 256), F32), v((4, 4, 64, 128), F32), v((4, 4, 64, 128), F32),
            v((4, 4, 4, 64, 128), BF), v((4, 3, 4, 64, 128), BF),
            v((3, 4, 64, 128), F32), v((3, 4, 64, 128), F32),
            v((3, 4, 4, 64, 128), BF), v((3, 4, 4, 64, 128), BF), v((3, 4, 64, 128), F32),
            v((2, 4, 64, 128), F32), v((2, 3, 64, 128), F32),
            pltpu.SemaphoreType.DMA((N_SEMS,)), pltpu.SemaphoreType.DMA((N_SEMS,)),
        ],
        compiler_params=pltpu.CompilerParams(
            collective_id=0, has_side_effects=True, vmem_limit_bytes=62 * 1024 * 1024),
        cost_estimate=pl.CostEstimate(flops=2 ** 31, bytes_accessed=5 * 2 ** 20, transcendentals=2 ** 20),
    )(target_logits, draft_hidden.transpose(0, 2, 1), draft_head, block_map.reshape(1, 256))
    return grad.transpose(0, 2, 1), loss


def solution(mesh):
    return jax.shard_map(
        on_device,
        mesh=mesh,
        in_specs=(P("tok", "vocab"), P(None, "tok", "vocab"), P("vocab", None), P()),
        out_specs=(P(None, "tok", "vocab"), P(None, ("tok", "vocab"))),
        check_vma=False,
    )
```

```python
import jax
import jax.numpy as jnp
from jax import lax
from jax.experimental import pallas as pl
from jax.experimental.pallas import tpu as pltpu
from jax.sharding import PartitionSpec as P

BF = jnp.bfloat16
F32 = jnp.float32
I32 = jnp.int32
MESH = pl.DeviceIdType.MESH

COUNTS = dict(AG1=3, A2A1=1, LSX=3, LSZ=15, LSN=1, AG2=4, AGX=12, A2A2=1, NBR=1, STX=3, STZ=15, LOX=3, LOZ=15, LOS=1,
              RSX=12, RSN=4, RSZ=4, RSY=3, RSS=6, HEAD=1, TL=1, HID=2, MAP=1)
BASE = {}
N_SEMS = 0
for _name, _count in COUNTS.items():
    BASE[_name] = N_SEMS
    N_SEMS += _count
AG1, A2A1, LSX, LSZ, LSN, AG2, AGX, A2A2, NBR, STX, STZ, LOX, LOZ, LOS, RSX, RSN, RSZ, RSY, RSS, HEAD, TL, HID, MAP = BASE.values()


def nt(a, b):
    return lax.dot_general(a, b, (((1,), (1,)), ((), ())), preferred_element_type=F32)


def mm(a, b):
    return lax.dot_general(a, b, (((1,), (0,)), ((), ())), preferred_element_type=F32)


def onehot(mask):
    return jnp.where(mask, 1.0, 0.0).astype(BF)


def combine_target(packs):
    top = packs[0][0:1]
    for p in packs[1:]:
        top = jnp.maximum(top, p[0:1])
    sums = jnp.zeros((2, 128), F32)
    for p in packs:
        sums += p[1:3] * jnp.exp(p[0:1] - top)
    return jnp.concatenate([top, sums, jnp.zeros((5, 128), F32)], axis=0)


def combine(packs):
    top = packs[0][0:2]
    for p in packs[1:]:
        top = jnp.maximum(top, p[0:2])
    total = jnp.zeros((2, 128), F32)
    for p in packs:
        total += p[2:4] * jnp.exp(p[0:2] - top)
    return jnp.concatenate([top, total], axis=0)


def kernel(tl_hbm, hid_hbm, head_hbm, bmap_hbm, grad_out, loss_out,
           bmap, tl, head, head_t, xt, send1, recv1, send2, recv2, pick_sel, place, logits, probs,
           lsx_send, lsx_recv, lsz_send, lsz_recv, lse_send, lse_recv, nbr_send, nbr_recv,
           stx_send, stx_recv, stz_send, stz_recv,
           lox_send, lox_recv, loz_send, loz_recv, los_send, los_recv, wide, own, own_z,
           rsx_send, rsx_recv, rsn_send, rsn_recv, rsz_send, rsz_recv, rsy_recv, rss_send, far_send, rss_recv, s_sem, r_sem):
    v = lax.axis_index("vocab")
    t = lax.axis_index("tok")
    z = v // 4
    x = lax.rem(v, 4)
    a = z // 4
    b = lax.rem(z, 4)

    def at_z(off):
        return (lax.rem(z + off + 16, 16) * 4 + x, t)

    def at_x(off):
        return (z * 4 + lax.rem(x + off, 4), t)

    before = (v, lax.rem(t + 7, 8))
    after = (v, lax.rem(t + 1, 8))

    def copy(k, src, dst, dev):
        return pltpu.make_async_remote_copy(
            src_ref=src, dst_ref=dst, send_sem=s_sem.at[k], recv_sem=r_sem.at[k],
            device_id=dev, device_id_type=MESH)

    sent = []

    def send(k, src, dst, dev):
        c = copy(k, src, dst, dev)
        c.start()
        sent.append(c)
        return c

    hid_copies = [pltpu.make_async_copy(hid_hbm.at[s], xt.at[a, b, x, :, pl.ds(s * 128, 128)], r_sem.at[HID + s])
                  for s in range(2)]
    for c in hid_copies:
        c.start()
    map_copy = pltpu.make_async_copy(bmap_hbm, bmap, r_sem.at[MAP])
    map_copy.start()
    tl_copy = pltpu.make_async_copy(tl_hbm, tl, r_sem.at[TL])
    tl_copy.start()
    head_copy = pltpu.make_async_copy(head_hbm, head, r_sem.at[HEAD])
    head_copy.start()

    barrier = pltpu.get_barrier_semaphore()

    def greet(i, c):
        pl.semaphore_signal(barrier, 1, device_id=(lax.rem(v + i, 64), t), device_id_type=MESH)
        return c

    lax.fori_loop(1, 64, greet, 0)
    pl.semaphore_signal(barrier, 1, device_id=before, device_id_type=MESH)
    pl.semaphore_signal(barrier, 1, device_id=after, device_id_type=MESH)

    map_copy.wait()
    bm_row = bmap[...]
    own_row = bm_row // 16
    loc_row = (bm_row - own_row * 16).astype(F32)
    own_row = own_row.astype(F32)
    sub = lax.broadcasted_iota(I32, (256, 256), 0)
    lane = lax.broadcasted_iota(I32, (256, 256), 1)
    own_all = jnp.broadcast_to(own_row, (256, 256))
    own_col = jnp.sum(jnp.where(sub == lane, own_all, 0.0), axis=1, keepdims=True)
    rank_row = jnp.sum(jnp.where((own_col == own_all) & (sub < lane), 1.0, 0.0), axis=0, keepdims=True)
    place_row = own_row * 16.0 + rank_row * 2.0
    row16 = lax.broadcasted_iota(I32, (16, 256), 0)
    mine = (jnp.broadcast_to(own_row, (16, 256)) == v.astype(F32)) & (
        jnp.broadcast_to(rank_row, (16, 256)) == (row16 // 2).astype(F32))
    found = jnp.sum(jnp.where(mine, 1.0, 0.0), axis=1, keepdims=True)
    block = jnp.sum(jnp.where(mine, jnp.broadcast_to(loc_row, (16, 256)), 0.0), axis=1, keepdims=True)
    odd = lax.rem(lax.broadcasted_iota(I32, (16, 1), 0), 2)
    mapped = jnp.max(jnp.where((jnp.broadcast_to(own_row, (16, 256)) == v.astype(F32)) & (
        jnp.broadcast_to(loc_row, (16, 256)) == row16.astype(F32)), 1.0, 0.0), axis=1, keepdims=True)
    first = jnp.where(found > 0.0, block.astype(I32) * 128 + odd, -4096)
    away = lax.broadcasted_iota(I32, (16, 2048), 1) - first

    def targets():
        top = tl[:, 0:128].astype(F32)
        for k in range(1, 16):
            top = jnp.maximum(top, tl[:, k * 128:(k + 1) * 128].astype(F32))
        top_col = jnp.max(top, axis=1, keepdims=True)
        total = jnp.zeros((128, 128), F32)
        kept = jnp.zeros((128, 128), F32)
        for k in range(16):
            weight = jnp.exp(tl[:, k * 128:(k + 1) * 128].astype(F32) - top_col)
            total += weight
            kept += weight * mapped[k:k + 1, :]
        t_max = jnp.max(top.T, axis=0, keepdims=True)
        t_sum = jnp.sum(total.T, axis=0, keepdims=True)
        t_kept = jnp.sum(kept.T, axis=0, keepdims=True)
        lsx_send[...] = jnp.concatenate([t_max, t_sum, t_kept, jnp.zeros((5, 128), F32)], axis=0)
    def targets_send():
        return [send(LSX + j - 1, lsx_send, lsx_recv.at[j - 1], at_x(j)) for j in range(1, 4)]

    def picks():
        def pick1(g, c):
            sel = jnp.concatenate([onehot(away == 2 * (8 * g + k)) for k in range(8)], axis=0)
            send1[pl.ds(8 * g, 8)] = nt(sel, tl[...]).astype(BF).reshape(8, 16, 128)
            return c

        lax.fori_loop(0, 8, pick1, 0)

    for c in hid_copies:
        c.wait()
    pl.semaphore_wait(barrier, 65)

    for j in range(1, 4):
        mine_xt = xt.at[a, b, x]
        send(AG1 + j - 1, mine_xt, mine_xt, at_z(4 * j))

    def spread():
        def spread1(i, c):
            p = lax.rem(v + i, 64)
            copy(A2A1, send1.at[p], recv1.at[v], (p, t)).start()
            return c

        lax.fori_loop(1, 64, spread1, 0)
        pltpu.make_async_copy(send1.at[v], recv1.at[v], r_sem.at[A2A1]).start()

    tl_copy.wait()
    targets()
    lsx = targets_send()
    picks()

    def got_x(ref_of, k, dev):
        copy(k, ref_of, ref_of, dev).wait_recv()

    def along_x(o):
        bb = lax.rem(b + o, 4)
        for j in range(1, 4):
            ref = xt.at[:, bb, x]
            send(AGX + 3 * o + j - 1, ref, ref, at_x(j))

    ag1 = [copy(AG1 + j - 1, xt.at[lax.rem(a + 4 - j, 4), b, x], xt.at[lax.rem(a + 4 - j, 4), b, x], at_z(4))
           for j in range(1, 4)]
    for c in ag1:
        c.wait_recv()
    send(AG2, xt.at[:, b, x], xt.at[:, b, x], at_z(1))
    send(AG2 + 1, xt.at[:, b, x], xt.at[:, b, x], at_z(-1))
    send(AG2 + 2, xt.at[pl.ds(0, 2), b, x], xt.at[pl.ds(0, 2), b, x], at_z(-2))
    send(AG2 + 3, xt.at[pl.ds(2, 2), b, x], xt.at[pl.ds(2, 2), b, x], at_z(2))
    along_x(0)

    for c in lsx:
        c.wait_recv()
    lsz_send[...] = combine_target([lsx_send[...]] + [lsx_recv[j] for j in range(3)])
    lsz = [send(LSZ + j - 1, lsz_send, lsz_recv.at[j - 1], at_z(j)) for j in range(1, 16)]

    r512 = lax.broadcasted_iota(I32, (512, 256), 0) // 2
    l512 = lax.broadcasted_iota(I32, (512, 256), 1)
    source = jnp.sum(jnp.where(r512 == l512, jnp.broadcast_to(place_row, (512, 256)), 0.0), axis=1, keepdims=True)
    source = source.astype(I32) + lax.rem(lax.broadcasted_iota(I32, (512, 1), 0), 2)
    pick_sel[...] = onehot(lax.broadcasted_iota(I32, (512, 1024), 1) == source)
    rr = lax.broadcasted_iota(I32, (512, 1), 0)
    goes = (lax.rem(rr, 128) // 2) * 8 + (rr // 128) * 2 + lax.rem(rr, 2)
    place[...] = onehot(lax.broadcasted_iota(I32, (512, 512), 1) == goes)

    b_prev = lax.rem(b + 3, 4)
    b_next = lax.rem(b + 1, 4)
    b_far = lax.rem(b + 2, 4)
    got_x(xt.at[:, b_prev, x], AG2, at_z(1))
    along_x(3)
    got_x(xt.at[:, b_next, x], AG2 + 1, at_z(1))
    along_x(1)
    got_x(xt.at[pl.ds(0, 2), b_far, x], AG2 + 2, at_z(1))
    got_x(xt.at[pl.ds(2, 2), b_far, x], AG2 + 3, at_z(1))
    along_x(2)
    spread()
    def exchange_again():
        pltpu.make_async_copy(recv1, recv1, r_sem.at[A2A1]).wait()
        send2[...] = mm(pick_sel[...], recv1[...].reshape(1024, 128)).reshape(64, 8, 128).astype(BF)

        def spread2(i, c):
            p = lax.rem(v + i, 64)
            copy(A2A2, send2.at[p], recv2.at[v], (p, t)).start()
            return c

        lax.fori_loop(1, 64, spread2, 0)
        pltpu.make_async_copy(send2.at[v], recv2.at[v], r_sem.at[A2A2]).start()

    head_copy.wait()
    eye256 = onehot(sub == lane)

    def turn(i, c):
        cols = pl.ds(pl.multiple_of(i * 256, 256), 256)
        head_t[cols, :] = nt(eye256, head[:, cols]).astype(BF)
        return c

    lax.fori_loop(0, 16, turn, 0)

    logits[...] = jnp.zeros((512, 256), F32)
    for o in (0, 3, 1, 2):
        if o == 2:
            exchange_again()
        bb = lax.rem(b + o, 4)
        for j in range(1, 4):
            ref = xt.at[:, bb, lax.rem(x + 4 - j, 4)]
            got_x(ref, AGX + 3 * o + j - 1, at_x(1))

        def forward(i, c):
            cols = pl.ds(pl.multiple_of((i * 4 + bb) * 256, 256), 256)
            logits[...] += mm(head[:, cols], xt[i, bb].reshape(256, 256))
            return c

        lax.fori_loop(0, 4, forward, 0)

    low = logits[...].astype(BF).astype(F32)
    d_max = jnp.max(low, axis=0, keepdims=True)
    d_sum = jnp.sum(jnp.exp(low - d_max), axis=0, keepdims=True)
    stx_send[...] = jnp.concatenate([d_max[:, 0:128], d_max[:, 128:], d_sum[:, 0:128], d_sum[:, 128:]], axis=0)
    stx = [send(STX + j - 1, stx_send, stx_recv.at[j - 1], at_x(j)) for j in range(1, 4)]
    for c in lsz:
        c.wait_recv()
    stat = combine_target([lsz_send[...]] + [lsz_recv[j] for j in range(15)])
    t_lse = stat[0:1] + jnp.log(stat[1:2])
    t_mass = stat[2:3] * jnp.exp(stat[0:1] - t_lse)
    lse_send[...] = jnp.concatenate([t_lse, t_mass, jnp.zeros((6, 128), F32)], axis=0)
    lse_copy = send(LSN, lse_send, lse_recv, before)

    for c in stx:
        c.wait_recv()
    stz_send[...] = combine([stx_send[...]] + [stx_recv[j] for j in range(3)])
    stz = [send(STZ + j - 1, stz_send, stz_recv.at[j - 1], at_z(j)) for j in range(1, 16)]

    pltpu.make_async_copy(recv2, recv2, r_sem.at[A2A2]).wait()
    picked = mm(place[...], recv2[...].reshape(512, 128)).astype(BF)
    r8 = lax.broadcasted_iota(I32, (8, 128), 0)
    l8 = lax.broadcasted_iota(I32, (8, 128), 1)
    nbr_send[...] = nt(onehot((r8 == 0) & (l8 == 0)), picked)
    nbr = send(NBR, nbr_send, nbr_recv, before)
    sub128 = lax.broadcasted_iota(I32, (128, 128), 0)
    lane128 = lax.broadcasted_iota(I32, (128, 128), 1)
    moved = mm(picked, onehot(sub128 == lane128 + 1))
    nbr.wait_recv()
    moved += lax.dot_general(
        nbr_recv[...].astype(BF), onehot((r8 == 0) & (l8 == 127)),
        (((0,), (0,)), ((), ())), preferred_element_type=F32)
    lse_copy.wait_recv()
    l1 = lax.broadcasted_iota(I32, (1, 128), 1)

    def with_next(k):
        row = lse_send[k:k + 1, :]
        late = jnp.where(l1 == 127, pltpu.roll(lse_recv[k:k + 1, :], 127, 1), pltpu.roll(row, 127, 1))
        return jnp.concatenate([row, late], axis=1)

    t_lse = with_next(0)
    mass = with_next(1)
    probs[...] = jnp.exp(jnp.concatenate([picked.astype(F32), moved], axis=1) - t_lse)

    for c in stz:
        c.wait_recv()
    stat = combine([stz_send[...]] + [stz_recv[j] for j in range(15)])
    d_lse = stat[0:2] + jnp.log(stat[2:4])

    d_lse = jnp.concatenate([d_lse[0:1], d_lse[1:2]], axis=1)
    l256 = lax.broadcasted_iota(I32, (1, 256), 1)
    keep = jnp.where((l256 == 255) & (t == 7), 0.0, 64.0)
    low = logits[...].astype(BF).astype(F32)
    grads = (keep * (mass * jnp.exp(low - d_lse) - probs[...])).astype(BF)

    loss = jnp.sum(probs[...] * (d_lse - logits[...].astype(BF).astype(F32)), axis=0, keepdims=True)
    lox_send[...] = jnp.concatenate([loss[:, 0:128], loss[:, 128:]], axis=0)
    lox = [send(LOX + j - 1, lox_send, lox_recv.at[j - 1], at_x(j)) for j in range(1, 4)]

    def along_x_back(o):
        for j in range(1, 4):
            send(RSX + 3 * o + j - 1, rsx_send.at[o, lax.rem(x + j, 4)], rsx_recv.at[o, j - 1], at_x(j))

    first_z = []
    for o in (1, 3, 2, 0):
        bb = lax.rem(b + o, 4)

        def backward(i, c):
            cols = pl.ds(pl.multiple_of((i * 4 + bb) * 256, 256), 256)
            part = mm(head_t[cols, :], grads).reshape(4, 64, 256)
            wide[...] = part
            own[o, i] = wide[x, :, 0:128]
            for k in range(4):
                rsx_send[o, k, i] = part[k, :, 0:128].astype(BF)
                if o == 0:
                    own_z[k, i] = part[k, :, 128:256]
                else:
                    rsz_send[o - 1, k, i] = part[k, :, 128:256].astype(BF)
            return c

        lax.fori_loop(0, 4, backward, 0)
        along_x_back(o)
        if o == 1:
            first_z.append(send(RSZ, rsz_send.at[0], rsz_recv.at[0], at_z(1)))
        elif o == 3:
            first_z.append(send(RSZ + 1, rsz_send.at[2], rsz_recv.at[2], at_z(-1)))
        elif o == 2:
            for k, part in ((0, pl.ds(0, 2)), (1, pl.ds(2, 2))):
                first_z.append(send(RSZ + 2 + k, rsz_send.at[1, :, part], rsz_recv.at[1, :, part], at_z(4 * k - 2)))

    def loss_on():
        for c in lox:
            c.wait_recv()
        loz_send[...] = lox_send[...] + lox_recv[0] + lox_recv[1] + lox_recv[2]
        return [send(LOZ + j - 1, loz_send, loz_recv.at[j - 1], at_z(j)) for j in range(1, 16)]

    def loss_over(loz):
        for c in loz:
            c.wait_recv()
        whole = loz_send[...]
        for j in range(15):
            whole += loz_recv[j]
        los_send[...] = jnp.concatenate([whole, jnp.zeros((6, 128), F32)], axis=0)
        return send(LOS, los_send, los_recv, after)
    def summed(o, into):
        for j in range(1, 4):
            ref = rsx_recv.at[o, j - 1]
            copy(RSX + 3 * o + j - 1, ref, ref, at_x(1)).wait_recv()

        def add(i, c):
            into[i] = own[o, i] + rsx_recv[o, 0, i].astype(F32) + rsx_recv[o, 1, i].astype(F32) + rsx_recv[o, 2, i].astype(F32)
            return c

        lax.fori_loop(0, 4, add, 0)

    def to_far(s, first, parts):
        def add_last(i, c):
            rss_send[s, i] = first(i) + parts[0, i] + parts[1, i] + parts[2, i]
            return c

        lax.fori_loop(0, 4, add_last, 0)
        def narrow(i, c):
            far_send[s, i] = rss_send[s, i].astype(BF)
            return c

        lax.fori_loop(0, 4, narrow, 0)
        return [send(RSS + 3 * s + j - 1, far_send.at[s, lax.rem(a + j, 4)], rss_recv.at[s, j - 1], at_z(4 * j))
                for j in range(1, 4)]

    loz = loss_on()
    near = []
    for o in (1, 3, 2):
        summed(o, rsn_send.at[o - 1])
        if o == 1:
            near.append(send(RSN, rsn_send.at[0], rsn_recv.at[0], at_z(1)))
        elif o == 3:
            near.append(send(RSN + 1, rsn_send.at[2], rsn_recv.at[2], at_z(-1)))
        else:
            for k, part in ((0, pl.ds(0, 2)), (1, pl.ds(2, 2))):
                near.append(send(RSN + 2 + k, rsn_send.at[1, part], rsn_recv.at[1, part], at_z(4 * k - 2)))
    for c in first_z:
        c.wait_recv()

    def add_z(i, c):
        for k in range(4):
            own_z[k, i] = (own_z[k, i] + rsz_recv[0, k, i].astype(F32) + rsz_recv[1, k, i].astype(F32)
                           + rsz_recv[2, k, i].astype(F32))
        return c

    lax.fori_loop(0, 4, add_z, 0)
    then_x = [send(RSY + j - 1, own_z.at[lax.rem(x + j, 4)], rsy_recv.at[j - 1], at_x(j)) for j in range(1, 4)]
    summed(0, rss_send.at[0])
    for c in near:
        c.wait_recv()
    far = to_far(0, lambda i: rss_send[0, i], rsn_recv)
    los = loss_over(loz)
    for c in then_x:
        c.wait_recv()
    far += to_far(1, lambda i: own_z[x, i], rsy_recv)

    los.wait_recv()
    here = los_send[...]
    other = los_recv[...]
    l8b = lax.broadcasted_iota(I32, (8, 128), 1)
    late = jnp.where(l8b == 0, jnp.where(t == 0, 0.0, pltpu.roll(other, 1, 1)), pltpu.roll(here, 1, 1))
    both = jnp.concatenate([here[0:1], late[1:2]], axis=0)
    l2 = lax.broadcasted_iota(I32, (2, 128), 1)
    for k in range(2):
        loss_out[:, k:k + 1] = jnp.sum(jnp.where(l2 == 2 * v + k, both, 0.0), axis=1, keepdims=True)

    for c in far:
        c.wait_recv()
    for s in range(2):
        grad_out[s] = (rss_send[s, a] + rss_recv[s, 0].astype(F32) + rss_recv[s, 1].astype(F32) + rss_recv[s, 2].astype(F32)).astype(BF)

    for c in sent:
        c.wait_send()
    for k, ref in ((A2A1, send1), (A2A2, send2)):
        most = ref.at[pl.ds(0, 63)]
        pltpu.make_async_copy(most, most, s_sem.at[k]).wait()


def on_device(target_logits, draft_hidden, draft_head, block_map):
    vm = pl.BlockSpec(memory_space=pltpu.VMEM)
    hbm = pl.BlockSpec(memory_space=pltpu.HBM)
    v = pltpu.VMEM
    tile = v((8, 128), F32)
    grad, loss = pl.pallas_call(
        kernel,
        name="draft_loss",
        out_shape=(jax.ShapeDtypeStruct((2, 64, 128), BF), jax.ShapeDtypeStruct((2, 2), F32)),
        in_specs=[hbm, hbm, hbm, hbm],
        out_specs=(vm, vm),
        scratch_shapes=[
            v((1, 256), I32), v((128, 2048), BF), v((512, 4096), BF), v((4096, 512), BF), v((4, 4, 4, 64, 256), BF),
            v((64, 16, 128), BF), v((64, 16, 128), BF), v((64, 8, 128), BF), v((64, 8, 128), BF),
            v((512, 1024), BF), v((512, 512), BF), v((512, 256), F32), v((512, 256), F32),
            tile, v((3, 8, 128), F32), tile, v((15, 8, 128), F32), tile, tile, v((8, 512), F32), v((8, 512), F32),
            v((4, 128), F32), v((3, 4, 128), F32), v((4, 128), F32), v((15, 4, 128), F32),
            v((2, 128), F32), v((3, 2, 128), F32), v((2, 128), F32), v((15, 2, 128), F32), tile, tile,
            v((4, 64, 256), F32), v((4, 4, 64, 128), F32), v((4, 4, 64, 128), F32),
            v((4, 4, 4, 64, 128), BF), v((4, 3, 4, 64, 128), BF),
            v((3, 4, 64, 128), F32), v((3, 4, 64, 128), F32),
            v((3, 4, 4, 64, 128), BF), v((3, 4, 4, 64, 128), BF), v((3, 4, 64, 128), F32),
            v((2, 4, 64, 128), F32), v((2, 4, 64, 128), BF), v((2, 3, 64, 128), BF),
            pltpu.SemaphoreType.DMA((N_SEMS,)), pltpu.SemaphoreType.DMA((N_SEMS,)),
        ],
        compiler_params=pltpu.CompilerParams(
            collective_id=0, has_side_effects=True, vmem_limit_bytes=62 * 1024 * 1024),
        cost_estimate=pl.CostEstimate(flops=2 ** 31, bytes_accessed=5 * 2 ** 20, transcendentals=2 ** 20),
    )(target_logits, draft_hidden.transpose(0, 2, 1), draft_head, block_map.reshape(1, 256))
    return grad.transpose(0, 2, 1), loss


def solution(mesh):
    return jax.shard_map(
        on_device,
        mesh=mesh,
        in_specs=(P("tok", "vocab"), P(None, "tok", "vocab"), P("vocab", None), P()),
        out_specs=(P(None, "tok", "vocab"), P(None, ("tok", "vocab"))),
        check_vma=False,
    )
```

```python
import jax
import jax.numpy as jnp
from jax import lax
from jax.experimental import pallas as pl
from jax.experimental.pallas import tpu as pltpu
from jax.sharding import PartitionSpec as P

BF = jnp.bfloat16
F32 = jnp.float32
I32 = jnp.int32
MESH = pl.DeviceIdType.MESH

COUNTS = dict(AG1=3, A2A1=1, LSX=3, LSZ=15, LSN=1, AG2=4, AGX=12, A2A2=1, NBR=1, STX=3, STZ=15, LOX=3, LOZ=15, LOS=1,
              RSX=12, RSN=4, RSZ=4, RSY=3, RSS=6, HEAD=1, TL=1, HID=2, MAP=1)
BASE = {}
N_SEMS = 0
for _name, _count in COUNTS.items():
    BASE[_name] = N_SEMS
    N_SEMS += _count
AG1, A2A1, LSX, LSZ, LSN, AG2, AGX, A2A2, NBR, STX, STZ, LOX, LOZ, LOS, RSX, RSN, RSZ, RSY, RSS, HEAD, TL, HID, MAP = BASE.values()


def nt(a, b):
    return lax.dot_general(a, b, (((1,), (1,)), ((), ())), preferred_element_type=F32)


def mm(a, b):
    return lax.dot_general(a, b, (((1,), (0,)), ((), ())), preferred_element_type=F32)


def onehot(mask):
    return jnp.where(mask, 1.0, 0.0).astype(BF)


def combine_target(packs):
    top = packs[0][0:1]
    for p in packs[1:]:
        top = jnp.maximum(top, p[0:1])
    sums = jnp.zeros((2, 128), F32)
    for p in packs:
        sums += p[1:3] * jnp.exp(p[0:1] - top)
    return jnp.concatenate([top, sums, jnp.zeros((5, 128), F32)], axis=0)


def combine(packs):
    top = packs[0][0:2]
    for p in packs[1:]:
        top = jnp.maximum(top, p[0:2])
    total = jnp.zeros((2, 128), F32)
    for p in packs:
        total += p[2:4] * jnp.exp(p[0:2] - top)
    return jnp.concatenate([top, total], axis=0)


def kernel(tl_hbm, hid_hbm, head_hbm, bmap_hbm, grad_out, loss_out,
           bmap, tl, head, head_t, xt, send1, recv1, send2, recv2, pick_sel, place, logits, probs,
           lsx_send, lsx_recv, lsz_send, lsz_recv, lse_send, lse_recv, nbr_send, nbr_recv,
           stx_send, stx_recv, stz_send, stz_recv,
           lox_send, lox_recv, loz_send, loz_recv, los_send, los_recv, wide, own, own_z,
           rsx_send, rsx_recv, rsn_send, rsn_recv, rsz_send, rsz_recv, rsy_recv, rss_send, far_send, rss_recv, s_sem, r_sem):
    v = lax.axis_index("vocab")
    t = lax.axis_index("tok")
    z = v // 4
    x = lax.rem(v, 4)
    a = z // 4
    b = lax.rem(z, 4)

    def at_z(off):
        return (lax.rem(z + off + 16, 16) * 4 + x, t)

    def at_x(off):
        return (z * 4 + lax.rem(x + off, 4), t)

    before = (v, lax.rem(t + 7, 8))
    after = (v, lax.rem(t + 1, 8))

    def copy(k, src, dst, dev):
        return pltpu.make_async_remote_copy(
            src_ref=src, dst_ref=dst, send_sem=s_sem.at[k], recv_sem=r_sem.at[k],
            device_id=dev, device_id_type=MESH)

    sent = []

    def send(k, src, dst, dev):
        c = copy(k, src, dst, dev)
        c.start()
        sent.append(c)
        return c

    hid_copies = [pltpu.make_async_copy(hid_hbm.at[s], xt.at[a, b, x, :, pl.ds(s * 128, 128)], r_sem.at[HID + s])
                  for s in range(2)]
    for c in hid_copies:
        c.start()
    map_copy = pltpu.make_async_copy(bmap_hbm, bmap, r_sem.at[MAP])
    map_copy.start()
    tl_copy = pltpu.make_async_copy(tl_hbm, tl, r_sem.at[TL])
    tl_copy.start()
    head_copy = pltpu.make_async_copy(head_hbm, head, r_sem.at[HEAD])
    head_copy.start()

    barrier = pltpu.get_barrier_semaphore()

    def greet(i, c):
        pl.semaphore_signal(barrier, 1, device_id=(lax.rem(v + i, 64), t), device_id_type=MESH)
        return c

    lax.fori_loop(1, 64, greet, 0)
    pl.semaphore_signal(barrier, 1, device_id=before, device_id_type=MESH)
    pl.semaphore_signal(barrier, 1, device_id=after, device_id_type=MESH)

    map_copy.wait()
    bm_row = bmap[...]
    own_row = bm_row // 16
    loc_row = (bm_row - own_row * 16).astype(F32)
    own_row = own_row.astype(F32)
    sub = lax.broadcasted_iota(I32, (256, 256), 0)
    lane = lax.broadcasted_iota(I32, (256, 256), 1)
    own_all = jnp.broadcast_to(own_row, (256, 256))
    own_col = jnp.sum(jnp.where(sub == lane, own_all, 0.0), axis=1, keepdims=True)
    rank_row = jnp.sum(jnp.where((own_col == own_all) & (sub < lane), 1.0, 0.0), axis=0, keepdims=True)
    place_row = own_row * 16.0 + rank_row * 2.0
    row16 = lax.broadcasted_iota(I32, (16, 256), 0)
    mine = (jnp.broadcast_to(own_row, (16, 256)) == v.astype(F32)) & (
        jnp.broadcast_to(rank_row, (16, 256)) == (row16 // 2).astype(F32))
    found = jnp.sum(jnp.where(mine, 1.0, 0.0), axis=1, keepdims=True)
    block = jnp.sum(jnp.where(mine, jnp.broadcast_to(loc_row, (16, 256)), 0.0), axis=1, keepdims=True)
    odd = lax.rem(lax.broadcasted_iota(I32, (16, 1), 0), 2)
    mapped = jnp.max(jnp.where((jnp.broadcast_to(own_row, (16, 256)) == v.astype(F32)) & (
        jnp.broadcast_to(loc_row, (16, 256)) == row16.astype(F32)), 1.0, 0.0), axis=1, keepdims=True)
    first = jnp.where(found > 0.0, block.astype(I32) * 128 + odd, -4096)
    away = lax.broadcasted_iota(I32, (16, 2048), 1) - first

    def targets():
        top = tl[:, 0:128].astype(F32)
        for k in range(1, 16):
            top = jnp.maximum(top, tl[:, k * 128:(k + 1) * 128].astype(F32))
        top_col = jnp.max(top, axis=1, keepdims=True)
        total = jnp.zeros((128, 128), F32)
        kept = jnp.zeros((128, 128), F32)
        for k in range(16):
            weight = jnp.exp(tl[:, k * 128:(k + 1) * 128].astype(F32) - top_col)
            total += weight
            kept += weight * mapped[k:k + 1, :]
        t_max = jnp.max(top.T, axis=0, keepdims=True)
        t_sum = jnp.sum(total.T, axis=0, keepdims=True)
        t_kept = jnp.sum(kept.T, axis=0, keepdims=True)
        lsx_send[...] = jnp.concatenate([t_max, t_sum, t_kept, jnp.zeros((5, 128), F32)], axis=0)
    def targets_send():
        return [send(LSX + j - 1, lsx_send, lsx_recv.at[j - 1], at_x(j)) for j in range(1, 4)]

    def picks():
        def pick1(g, c):
            sel = jnp.concatenate([onehot(away == 2 * (8 * g + k)) for k in range(8)], axis=0)
            send1[pl.ds(8 * g, 8)] = nt(sel, tl[...]).astype(BF).reshape(8, 16, 128)
            return c

        lax.fori_loop(0, 8, pick1, 0)

    for c in hid_copies:
        c.wait()
    pl.semaphore_wait(barrier, 65)

    for j in range(1, 4):
        mine_xt = xt.at[a, b, x]
        send(AG1 + j - 1, mine_xt, mine_xt, at_z(4 * j))

    def spread():
        def spread1(i, c):
            p = lax.rem(v + i, 64)
            copy(A2A1, send1.at[p], recv1.at[v], (p, t)).start()
            return c

        lax.fori_loop(1, 64, spread1, 0)
        pltpu.make_async_copy(send1.at[v], recv1.at[v], r_sem.at[A2A1]).start()

    tl_copy.wait()
    targets()
    lsx = targets_send()
    picks()

    def got_x(ref_of, k, dev):
        copy(k, ref_of, ref_of, dev).wait_recv()

    def along_x(o):
        bb = lax.rem(b + o, 4)
        for j in range(1, 4):
            ref = xt.at[:, bb, x]
            send(AGX + 3 * o + j - 1, ref, ref, at_x(j))

    ag1 = [copy(AG1 + j - 1, xt.at[lax.rem(a + 4 - j, 4), b, x], xt.at[lax.rem(a + 4 - j, 4), b, x], at_z(4))
           for j in range(1, 4)]
    for c in ag1:
        c.wait_recv()
    send(AG2, xt.at[:, b, x], xt.at[:, b, x], at_z(1))
    send(AG2 + 1, xt.at[:, b, x], xt.at[:, b, x], at_z(-1))
    send(AG2 + 2, xt.at[pl.ds(0, 2), b, x], xt.at[pl.ds(0, 2), b, x], at_z(-2))
    send(AG2 + 3, xt.at[pl.ds(2, 2), b, x], xt.at[pl.ds(2, 2), b, x], at_z(2))
    along_x(0)
    spread()

    for c in lsx:
        c.wait_recv()
    lsz_send[...] = combine_target([lsx_send[...]] + [lsx_recv[j] for j in range(3)])
    lsz = [send(LSZ + j - 1, lsz_send, lsz_recv.at[j - 1], at_z(j)) for j in range(1, 16)]

    r512 = lax.broadcasted_iota(I32, (512, 256), 0) // 2
    l512 = lax.broadcasted_iota(I32, (512, 256), 1)
    source = jnp.sum(jnp.where(r512 == l512, jnp.broadcast_to(place_row, (512, 256)), 0.0), axis=1, keepdims=True)
    source = source.astype(I32) + lax.rem(lax.broadcasted_iota(I32, (512, 1), 0), 2)
    pick_sel[...] = onehot(lax.broadcasted_iota(I32, (512, 1024), 1) == source)
    rr = lax.broadcasted_iota(I32, (512, 1), 0)
    goes = (lax.rem(rr, 128) // 2) * 8 + (rr // 128) * 2 + lax.rem(rr, 2)
    place[...] = onehot(lax.broadcasted_iota(I32, (512, 512), 1) == goes)

    b_prev = lax.rem(b + 3, 4)
    b_next = lax.rem(b + 1, 4)
    b_far = lax.rem(b + 2, 4)
    got_x(xt.at[:, b_prev, x], AG2, at_z(1))
    along_x(3)
    got_x(xt.at[:, b_next, x], AG2 + 1, at_z(1))
    along_x(1)
    got_x(xt.at[pl.ds(0, 2), b_far, x], AG2 + 2, at_z(1))
    got_x(xt.at[pl.ds(2, 2), b_far, x], AG2 + 3, at_z(1))
    along_x(2)
    def exchange_again():
        pltpu.make_async_copy(recv1, recv1, r_sem.at[A2A1]).wait()
        send2[...] = mm(pick_sel[...], recv1[...].reshape(1024, 128)).reshape(64, 8, 128).astype(BF)

        def spread2(i, c):
            p = lax.rem(v + i, 64)
            copy(A2A2, send2.at[p], recv2.at[v], (p, t)).start()
            return c

        lax.fori_loop(1, 64, spread2, 0)
        pltpu.make_async_copy(send2.at[v], recv2.at[v], r_sem.at[A2A2]).start()

    head_copy.wait()
    eye256 = onehot(sub == lane)

    def turn(i, c):
        cols = pl.ds(pl.multiple_of(i * 256, 256), 256)
        head_t[cols, :] = nt(eye256, head[:, cols]).astype(BF)
        return c

    lax.fori_loop(0, 16, turn, 0)

    logits[...] = jnp.zeros((512, 256), F32)
    for o in (0, 3, 1, 2):
        if o == 2:
            exchange_again()
        bb = lax.rem(b + o, 4)
        for j in range(1, 4):
            ref = xt.at[:, bb, lax.rem(x + 4 - j, 4)]
            got_x(ref, AGX + 3 * o + j - 1, at_x(1))

        def forward(i, c):
            cols = pl.ds(pl.multiple_of((i * 4 + bb) * 256, 256), 256)
            logits[...] += mm(head[:, cols], xt[i, bb].reshape(256, 256))
            return c

        lax.fori_loop(0, 4, forward, 0)

    low = logits[...].astype(BF).astype(F32)
    d_max = jnp.max(low, axis=0, keepdims=True)
    d_sum = jnp.sum(jnp.exp(low - d_max), axis=0, keepdims=True)
    stx_send[...] = jnp.concatenate([d_max[:, 0:128], d_max[:, 128:], d_sum[:, 0:128], d_sum[:, 128:]], axis=0)
    stx = [send(STX + j - 1, stx_send, stx_recv.at[j - 1], at_x(j)) for j in range(1, 4)]
    for c in lsz:
        c.wait_recv()
    stat = combine_target([lsz_send[...]] + [lsz_recv[j] for j in range(15)])
    t_lse = stat[0:1] + jnp.log(stat[1:2])
    t_mass = stat[2:3] * jnp.exp(stat[0:1] - t_lse)
    lse_send[...] = jnp.concatenate([t_lse, t_mass, jnp.zeros((6, 128), F32)], axis=0)
    lse_copy = send(LSN, lse_send, lse_recv, before)

    for c in stx:
        c.wait_recv()
    stz_send[...] = combine([stx_send[...]] + [stx_recv[j] for j in range(3)])
    stz = [send(STZ + j - 1, stz_send, stz_recv.at[j - 1], at_z(j)) for j in range(1, 16)]

    pltpu.make_async_copy(recv2, recv2, r_sem.at[A2A2]).wait()
    picked = mm(place[...], recv2[...].reshape(512, 128)).astype(BF)
    r8 = lax.broadcasted_iota(I32, (8, 128), 0)
    l8 = lax.broadcasted_iota(I32, (8, 128), 1)
    nbr_send[...] = nt(onehot((r8 == 0) & (l8 == 0)), picked)
    nbr = send(NBR, nbr_send, nbr_recv, before)
    sub128 = lax.broadcasted_iota(I32, (128, 128), 0)
    lane128 = lax.broadcasted_iota(I32, (128, 128), 1)
    moved = mm(picked, onehot(sub128 == lane128 + 1))
    nbr.wait_recv()
    moved += lax.dot_general(
        nbr_recv[...].astype(BF), onehot((r8 == 0) & (l8 == 127)),
        (((0,), (0,)), ((), ())), preferred_element_type=F32)
    lse_copy.wait_recv()
    l1 = lax.broadcasted_iota(I32, (1, 128), 1)

    def with_next(k):
        row = lse_send[k:k + 1, :]
        late = jnp.where(l1 == 127, pltpu.roll(lse_recv[k:k + 1, :], 127, 1), pltpu.roll(row, 127, 1))
        return jnp.concatenate([row, late], axis=1)

    t_lse = with_next(0)
    mass = with_next(1)
    probs[...] = jnp.exp(jnp.concatenate([picked.astype(F32), moved], axis=1) - t_lse)

    for c in stz:
        c.wait_recv()
    stat = combine([stz_send[...]] + [stz_recv[j] for j in range(15)])
    d_lse = stat[0:2] + jnp.log(stat[2:4])

    d_lse = jnp.concatenate([d_lse[0:1], d_lse[1:2]], axis=1)
    l256 = lax.broadcasted_iota(I32, (1, 256), 1)
    keep = jnp.where((l256 == 255) & (t == 7), 0.0, 64.0)
    low = logits[...].astype(BF).astype(F32)
    grads = (keep * (mass * jnp.exp(low - d_lse) - probs[...])).astype(BF)

    loss = jnp.sum(probs[...] * (d_lse - logits[...].astype(BF).astype(F32)), axis=0, keepdims=True)
    lox_send[...] = jnp.concatenate([loss[:, 0:128], loss[:, 128:]], axis=0)
    lox = [send(LOX + j - 1, lox_send, lox_recv.at[j - 1], at_x(j)) for j in range(1, 4)]

    def along_x_back(o):
        for j in range(1, 4):
            send(RSX + 3 * o + j - 1, rsx_send.at[o, lax.rem(x + j, 4)], rsx_recv.at[o, j - 1], at_x(j))

    first_z = []
    for o in (1, 3, 2, 0):
        bb = lax.rem(b + o, 4)

        def backward(i, c):
            cols = pl.ds(pl.multiple_of((i * 4 + bb) * 256, 256), 256)
            part = mm(head_t[cols, :], grads).reshape(4, 64, 256)
            wide[...] = part
            own[o, i] = wide[x, :, 0:128]
            for k in range(4):
                rsx_send[o, k, i] = part[k, :, 0:128].astype(BF)
                if o == 0:
                    own_z[k, i] = part[k, :, 128:256]
                else:
                    rsz_send[o - 1, k, i] = part[k, :, 128:256].astype(BF)
            return c

        lax.fori_loop(0, 4, backward, 0)
        if o == 1:
            first_z.append(send(RSZ, rsz_send.at[0], rsz_recv.at[0], at_z(1)))
        elif o == 3:
            first_z.append(send(RSZ + 1, rsz_send.at[2], rsz_recv.at[2], at_z(-1)))
        elif o == 2:
            for k, part in ((0, pl.ds(0, 2)), (1, pl.ds(2, 2))):
                first_z.append(send(RSZ + 2 + k, rsz_send.at[1, :, part], rsz_recv.at[1, :, part], at_z(4 * k - 2)))
        along_x_back(o)

    def loss_on():
        for c in lox:
            c.wait_recv()
        loz_send[...] = lox_send[...] + lox_recv[0] + lox_recv[1] + lox_recv[2]
        return [send(LOZ + j - 1, loz_send, loz_recv.at[j - 1], at_z(j)) for j in range(1, 16)]

    def loss_over(loz):
        for c in loz:
            c.wait_recv()
        whole = loz_send[...]
        for j in range(15):
            whole += loz_recv[j]
        los_send[...] = jnp.concatenate([whole, jnp.zeros((6, 128), F32)], axis=0)
        return send(LOS, los_send, los_recv, after)
    def summed(o, into):
        for j in range(1, 4):
            ref = rsx_recv.at[o, j - 1]
            copy(RSX + 3 * o + j - 1, ref, ref, at_x(1)).wait_recv()

        def add(i, c):
            into[i] = own[o, i] + rsx_recv[o, 0, i].astype(F32) + rsx_recv[o, 1, i].astype(F32) + rsx_recv[o, 2, i].astype(F32)
            return c

        lax.fori_loop(0, 4, add, 0)

    def far_copy(s, k):
        i = k + jnp.where(a <= k, 1, 0)
        j = lax.rem(i + 4 - a, 4)
        return send(RSS + 3 * s + j - 1, far_send.at[s, i], rss_recv.at[s, j - 1], ((i * 4 + b) * 4 + x, t))

    def to_far(s, first, parts):
        def add_last(i, c):
            rss_send[s, i] = first(i) + parts[0, i] + parts[1, i] + parts[2, i]
            return c

        lax.fori_loop(0, 4, add_last, 0)
        def narrow(i, c):
            far_send[s, i] = rss_send[s, i].astype(BF)
            return c

        lax.fori_loop(0, 4, narrow, 0)
        return [far_copy(s, k) for k in range(3)]

    loz = loss_on()
    near = []
    for o in (1, 3, 2):
        summed(o, rsn_send.at[o - 1])
        if o == 1:
            near.append(send(RSN, rsn_send.at[0], rsn_recv.at[0], at_z(1)))
        elif o == 3:
            near.append(send(RSN + 1, rsn_send.at[2], rsn_recv.at[2], at_z(-1)))
        else:
            for k, part in ((0, pl.ds(0, 2)), (1, pl.ds(2, 2))):
                near.append(send(RSN + 2 + k, rsn_send.at[1, part], rsn_recv.at[1, part], at_z(4 * k - 2)))
    for c in first_z:
        c.wait_recv()

    def add_z(i, c):
        for k in range(4):
            own_z[k, i] = (own_z[k, i] + rsz_recv[0, k, i].astype(F32) + rsz_recv[1, k, i].astype(F32)
                           + rsz_recv[2, k, i].astype(F32))
        return c

    lax.fori_loop(0, 4, add_z, 0)
    then_x = [send(RSY + j - 1, own_z.at[lax.rem(x + j, 4)], rsy_recv.at[j - 1], at_x(j)) for j in range(1, 4)]
    summed(0, rss_send.at[0])
    for c in near:
        c.wait_recv()
    far = to_far(0, lambda i: rss_send[0, i], rsn_recv)
    los = loss_over(loz)
    for c in then_x:
        c.wait_recv()
    far += to_far(1, lambda i: own_z[x, i], rsy_recv)

    los.wait_recv()
    here = los_send[...]
    other = los_recv[...]
    l8b = lax.broadcasted_iota(I32, (8, 128), 1)
    late = jnp.where(l8b == 0, jnp.where(t == 0, 0.0, pltpu.roll(other, 1, 1)), pltpu.roll(here, 1, 1))
    both = jnp.concatenate([here[0:1], late[1:2]], axis=0)
    l2 = lax.broadcasted_iota(I32, (2, 128), 1)
    for k in range(2):
        loss_out[:, k:k + 1] = jnp.sum(jnp.where(l2 == 2 * v + k, both, 0.0), axis=1, keepdims=True)

    for c in far:
        c.wait_recv()
    for s in range(2):
        grad_out[s] = (rss_send[s, a] + rss_recv[s, 0].astype(F32) + rss_recv[s, 1].astype(F32) + rss_recv[s, 2].astype(F32)).astype(BF)

    for c in sent:
        c.wait_send()
    for k, ref in ((A2A1, send1), (A2A2, send2)):
        most = ref.at[pl.ds(0, 63)]
        pltpu.make_async_copy(most, most, s_sem.at[k]).wait()


def on_device(target_logits, draft_hidden, draft_head, block_map):
    vm = pl.BlockSpec(memory_space=pltpu.VMEM)
    hbm = pl.BlockSpec(memory_space=pltpu.HBM)
    v = pltpu.VMEM
    tile = v((8, 128), F32)
    grad, loss = pl.pallas_call(
        kernel,
        name="draft_loss",
        out_shape=(jax.ShapeDtypeStruct((2, 64, 128), BF), jax.ShapeDtypeStruct((2, 2), F32)),
        in_specs=[hbm, hbm, hbm, hbm],
        out_specs=(vm, vm),
        scratch_shapes=[
            v((1, 256), I32), v((128, 2048), BF), v((512, 4096), BF), v((4096, 512), BF), v((4, 4, 4, 64, 256), BF),
            v((64, 16, 128), BF), v((64, 16, 128), BF), v((64, 8, 128), BF), v((64, 8, 128), BF),
            v((512, 1024), BF), v((512, 512), BF), v((512, 256), F32), v((512, 256), F32),
            tile, v((3, 8, 128), F32), tile, v((15, 8, 128), F32), tile, tile, v((8, 512), F32), v((8, 512), F32),
            v((4, 128), F32), v((3, 4, 128), F32), v((4, 128), F32), v((15, 4, 128), F32),
            v((2, 128), F32), v((3, 2, 128), F32), v((2, 128), F32), v((15, 2, 128), F32), tile, tile,
            v((4, 64, 256), F32), v((4, 4, 64, 128), F32), v((4, 4, 64, 128), F32),
            v((4, 4, 4, 64, 128), BF), v((4, 3, 4, 64, 128), BF),
            v((3, 4, 64, 128), F32), v((3, 4, 64, 128), F32),
            v((3, 4, 4, 64, 128), BF), v((3, 4, 4, 64, 128), BF), v((3, 4, 64, 128), F32),
            v((2, 4, 64, 128), F32), v((2, 4, 64, 128), BF), v((2, 3, 64, 128), BF),
            pltpu.SemaphoreType.DMA((N_SEMS,)), pltpu.SemaphoreType.DMA((N_SEMS,)),
        ],
        compiler_params=pltpu.CompilerParams(
            collective_id=0, has_side_effects=True, vmem_limit_bytes=62 * 1024 * 1024),
        cost_estimate=pl.CostEstimate(flops=2 ** 31, bytes_accessed=5 * 2 ** 20, transcendentals=2 ** 20),
    )(target_logits, draft_hidden.transpose(0, 2, 1), draft_head, block_map.reshape(1, 256))
    return grad.transpose(0, 2, 1), loss


def solution(mesh):
    return jax.shard_map(
        on_device,
        mesh=mesh,
        in_specs=(P("tok", "vocab"), P(None, "tok", "vocab"), P("vocab", None), P()),
        out_specs=(P(None, "tok", "vocab"), P(None, ("tok", "vocab"))),
        check_vma=False,
    )
```

```python
import jax
import jax.numpy as jnp
from jax import lax
from jax.experimental import pallas as pl
from jax.experimental.pallas import tpu as pltpu
from jax.sharding import PartitionSpec as P

BF = jnp.bfloat16
F32 = jnp.float32
I32 = jnp.int32
MESH = pl.DeviceIdType.MESH

COUNTS = dict(AG1=3, A2A1=1, LSX=3, LSZ=15, LSN=1, AG2=4, AGX=12, A2A2=1, NBR=1, STX=3, STZ=15, LOX=3, LOZ=15, LOS=1,
              RSX=12, RSN=4, RSZ=4, RSY=3, RSS=6, HEAD=1, TL=1, HID=2, MAP=1)
BASE = {}
N_SEMS = 0
for _name, _count in COUNTS.items():
    BASE[_name] = N_SEMS
    N_SEMS += _count
AG1, A2A1, LSX, LSZ, LSN, AG2, AGX, A2A2, NBR, STX, STZ, LOX, LOZ, LOS, RSX, RSN, RSZ, RSY, RSS, HEAD, TL, HID, MAP = BASE.values()


def nt(a, b):
    return lax.dot_general(a, b, (((1,), (1,)), ((), ())), preferred_element_type=F32)


def mm(a, b):
    return lax.dot_general(a, b, (((1,), (0,)), ((), ())), preferred_element_type=F32)


def onehot(mask):
    return jnp.where(mask, 1.0, 0.0).astype(BF)


def combine_target(packs):
    top = packs[0][0:1]
    for p in packs[1:]:
        top = jnp.maximum(top, p[0:1])
    sums = jnp.zeros((2, 128), F32)
    for p in packs:
        sums += p[1:3] * jnp.exp(p[0:1] - top)
    return jnp.concatenate([top, sums, jnp.zeros((5, 128), F32)], axis=0)


def combine(packs):
    top = packs[0][0:2]
    for p in packs[1:]:
        top = jnp.maximum(top, p[0:2])
    total = jnp.zeros((2, 128), F32)
    for p in packs:
        total += p[2:4] * jnp.exp(p[0:2] - top)
    return jnp.concatenate([top, total], axis=0)


def kernel(tl_hbm, hid_hbm, head_hbm, bmap_hbm, grad_out, loss_out,
           bmap, tl, head, head_t, xt, send1, recv1, send2, recv2, pick_sel, place, logits, probs,
           lsx_send, lsx_recv, lsz_send, lsz_recv, lse_send, lse_recv, nbr_send, nbr_recv,
           stx_send, stx_recv, stz_send, stz_recv,
           lox_send, lox_recv, loz_send, loz_recv, los_send, los_recv, wide, own, own_z,
           rsx_send, rsx_recv, rsn_send, rsn_recv, rsz_send, rsz_recv, rsy_recv, rss_send, far_send, rss_recv, s_sem, r_sem):
    v = lax.axis_index("vocab")
    t = lax.axis_index("tok")
    z = v // 4
    x = lax.rem(v, 4)
    a = z // 4
    b = lax.rem(z, 4)

    def at_z(off):
        return (lax.rem(z + off + 16, 16) * 4 + x, t)

    def at_x(off):
        return (z * 4 + lax.rem(x + off, 4), t)

    before = (v, lax.rem(t + 7, 8))
    after = (v, lax.rem(t + 1, 8))

    def copy(k, src, dst, dev):
        return pltpu.make_async_remote_copy(
            src_ref=src, dst_ref=dst, send_sem=s_sem.at[k], recv_sem=r_sem.at[k],
            device_id=dev, device_id_type=MESH)

    def both_ways(i):
        half = i // 2
        return lax.rem(v + jnp.where(i - 2 * half == 1, half + 1, 64 - half), 64)

    sent = []

    def send(k, src, dst, dev):
        c = copy(k, src, dst, dev)
        c.start()
        sent.append(c)
        return c

    hid_copies = [pltpu.make_async_copy(hid_hbm.at[s], xt.at[a, b, x, :, pl.ds(s * 128, 128)], r_sem.at[HID + s])
                  for s in range(2)]
    for c in hid_copies:
        c.start()
    map_copy = pltpu.make_async_copy(bmap_hbm, bmap, r_sem.at[MAP])
    map_copy.start()
    tl_copy = pltpu.make_async_copy(tl_hbm, tl, r_sem.at[TL])
    tl_copy.start()
    head_copy = pltpu.make_async_copy(head_hbm, head, r_sem.at[HEAD])
    head_copy.start()

    barrier = pltpu.get_barrier_semaphore()

    def greet(i, c):
        pl.semaphore_signal(barrier, 1, device_id=(lax.rem(v + i, 64), t), device_id_type=MESH)
        return c

    lax.fori_loop(1, 64, greet, 0)
    pl.semaphore_signal(barrier, 1, device_id=before, device_id_type=MESH)
    pl.semaphore_signal(barrier, 1, device_id=after, device_id_type=MESH)

    map_copy.wait()
    bm_row = bmap[...]
    own_row = bm_row // 16
    loc_row = (bm_row - own_row * 16).astype(F32)
    own_row = own_row.astype(F32)
    sub = lax.broadcasted_iota(I32, (256, 256), 0)
    lane = lax.broadcasted_iota(I32, (256, 256), 1)
    own_all = jnp.broadcast_to(own_row, (256, 256))
    own_col = jnp.sum(jnp.where(sub == lane, own_all, 0.0), axis=1, keepdims=True)
    rank_row = jnp.sum(jnp.where((own_col == own_all) & (sub < lane), 1.0, 0.0), axis=0, keepdims=True)
    place_row = own_row * 16.0 + rank_row * 2.0
    row16 = lax.broadcasted_iota(I32, (16, 256), 0)
    mine = (jnp.broadcast_to(own_row, (16, 256)) == v.astype(F32)) & (
        jnp.broadcast_to(rank_row, (16, 256)) == (row16 // 2).astype(F32))
    found = jnp.sum(jnp.where(mine, 1.0, 0.0), axis=1, keepdims=True)
    block = jnp.sum(jnp.where(mine, jnp.broadcast_to(loc_row, (16, 256)), 0.0), axis=1, keepdims=True)
    odd = lax.rem(lax.broadcasted_iota(I32, (16, 1), 0), 2)
    mapped = jnp.max(jnp.where((jnp.broadcast_to(own_row, (16, 256)) == v.astype(F32)) & (
        jnp.broadcast_to(loc_row, (16, 256)) == row16.astype(F32)), 1.0, 0.0), axis=1, keepdims=True)
    first = jnp.where(found > 0.0, block.astype(I32) * 128 + odd, -4096)
    away = lax.broadcasted_iota(I32, (16, 2048), 1) - first

    def targets():
        top = tl[:, 0:128].astype(F32)
        for k in range(1, 16):
            top = jnp.maximum(top, tl[:, k * 128:(k + 1) * 128].astype(F32))
        top_col = jnp.max(top, axis=1, keepdims=True)
        total = jnp.zeros((128, 128), F32)
        kept = jnp.zeros((128, 128), F32)
        for k in range(16):
            weight = jnp.exp(tl[:, k * 128:(k + 1) * 128].astype(F32) - top_col)
            total += weight
            kept += weight * mapped[k:k + 1, :]
        t_max = jnp.max(top.T, axis=0, keepdims=True)
        t_sum = jnp.sum(total.T, axis=0, keepdims=True)
        t_kept = jnp.sum(kept.T, axis=0, keepdims=True)
        lsx_send[...] = jnp.concatenate([t_max, t_sum, t_kept, jnp.zeros((5, 128), F32)], axis=0)
    def targets_send():
        return [send(LSX + j - 1, lsx_send, lsx_recv.at[j - 1], at_x(j)) for j in range(1, 4)]

    def picks():
        def pick1(g, c):
            sel = jnp.concatenate([onehot(away == 2 * (8 * g + k)) for k in range(8)], axis=0)
            send1[pl.ds(8 * g, 8)] = nt(sel, tl[...]).astype(BF).reshape(8, 16, 128)
            return c

        lax.fori_loop(0, 8, pick1, 0)

    for c in hid_copies:
        c.wait()
    pl.semaphore_wait(barrier, 65)

    for j in range(1, 4):
        mine_xt = xt.at[a, b, x]
        send(AG1 + j - 1, mine_xt, mine_xt, at_z(4 * j))

    def spread():
        def spread1(i, c):
            p = both_ways(i)
            copy(A2A1, send1.at[p], recv1.at[v], (p, t)).start()
            return c

        lax.fori_loop(1, 64, spread1, 0)
        pltpu.make_async_copy(send1.at[v], recv1.at[v], r_sem.at[A2A1]).start()

    tl_copy.wait()
    targets()
    lsx = targets_send()
    picks()

    def got_x(ref_of, k, dev):
        copy(k, ref_of, ref_of, dev).wait_recv()

    def along_x(o):
        bb = lax.rem(b + o, 4)
        for j in range(1, 4):
            ref = xt.at[:, bb, x]
            send(AGX + 3 * o + j - 1, ref, ref, at_x(j))

    ag1 = [copy(AG1 + j - 1, xt.at[lax.rem(a + 4 - j, 4), b, x], xt.at[lax.rem(a + 4 - j, 4), b, x], at_z(4))
           for j in range(1, 4)]
    for c in ag1:
        c.wait_recv()
    send(AG2, xt.at[:, b, x], xt.at[:, b, x], at_z(1))
    send(AG2 + 1, xt.at[:, b, x], xt.at[:, b, x], at_z(-1))
    send(AG2 + 2, xt.at[pl.ds(0, 2), b, x], xt.at[pl.ds(0, 2), b, x], at_z(-2))
    send(AG2 + 3, xt.at[pl.ds(2, 2), b, x], xt.at[pl.ds(2, 2), b, x], at_z(2))
    along_x(0)
    spread()

    for c in lsx:
        c.wait_recv()
    lsz_send[...] = combine_target([lsx_send[...]] + [lsx_recv[j] for j in range(3)])
    lsz = [send(LSZ + j - 1, lsz_send, lsz_recv.at[j - 1], at_z(j)) for j in range(1, 16)]

    r512 = lax.broadcasted_iota(I32, (512, 256), 0) // 2
    l512 = lax.broadcasted_iota(I32, (512, 256), 1)
    source = jnp.sum(jnp.where(r512 == l512, jnp.broadcast_to(place_row, (512, 256)), 0.0), axis=1, keepdims=True)
    source = source.astype(I32) + lax.rem(lax.broadcasted_iota(I32, (512, 1), 0), 2)
    pick_sel[...] = onehot(lax.broadcasted_iota(I32, (512, 1024), 1) == source)
    rr = lax.broadcasted_iota(I32, (512, 1), 0)
    goes = (lax.rem(rr, 128) // 2) * 8 + (rr // 128) * 2 + lax.rem(rr, 2)
    place[...] = onehot(lax.broadcasted_iota(I32, (512, 512), 1) == goes)

    b_prev = lax.rem(b + 3, 4)
    b_next = lax.rem(b + 1, 4)
    b_far = lax.rem(b + 2, 4)
    got_x(xt.at[:, b_prev, x], AG2, at_z(1))
    along_x(3)
    got_x(xt.at[:, b_next, x], AG2 + 1, at_z(1))
    along_x(1)
    got_x(xt.at[pl.ds(0, 2), b_far, x], AG2 + 2, at_z(1))
    got_x(xt.at[pl.ds(2, 2), b_far, x], AG2 + 3, at_z(1))
    along_x(2)
    def exchange_again():
        pltpu.make_async_copy(recv1, recv1, r_sem.at[A2A1]).wait()
        send2[...] = mm(pick_sel[...], recv1[...].reshape(1024, 128)).reshape(64, 8, 128).astype(BF)

        def spread2(i, c):
            p = both_ways(i)
            copy(A2A2, send2.at[p], recv2.at[v], (p, t)).start()
            return c

        lax.fori_loop(1, 64, spread2, 0)
        pltpu.make_async_copy(send2.at[v], recv2.at[v], r_sem.at[A2A2]).start()

    head_copy.wait()
    eye256 = onehot(sub == lane)

    def turn(i, c):
        cols = pl.ds(pl.multiple_of(i * 256, 256), 256)
        head_t[cols, :] = nt(eye256, head[:, cols]).astype(BF)
        return c

    lax.fori_loop(0, 16, turn, 0)

    logits[...] = jnp.zeros((512, 256), F32)
    for o in (0, 3, 1, 2):
        if o == 2:
            exchange_again()
        bb = lax.rem(b + o, 4)
        for j in range(1, 4):
            ref = xt.at[:, bb, lax.rem(x + 4 - j, 4)]
            got_x(ref, AGX + 3 * o + j - 1, at_x(1))

        def forward(i, c):
            cols = pl.ds(pl.multiple_of((i * 4 + bb) * 256, 256), 256)
            logits[...] += mm(head[:, cols], xt[i, bb].reshape(256, 256))
            return c

        lax.fori_loop(0, 4, forward, 0)

    low = logits[...].astype(BF).astype(F32)
    d_max = jnp.max(low, axis=0, keepdims=True)
    d_sum = jnp.sum(jnp.exp(low - d_max), axis=0, keepdims=True)
    stx_send[...] = jnp.concatenate([d_max[:, 0:128], d_max[:, 128:], d_sum[:, 0:128], d_sum[:, 128:]], axis=0)
    stx = [send(STX + j - 1, stx_send, stx_recv.at[j - 1], at_x(j)) for j in range(1, 4)]
    for c in lsz:
        c.wait_recv()
    stat = combine_target([lsz_send[...]] + [lsz_recv[j] for j in range(15)])
    t_lse = stat[0:1] + jnp.log(stat[1:2])
    t_mass = stat[2:3] * jnp.exp(stat[0:1] - t_lse)
    lse_send[...] = jnp.concatenate([t_lse, t_mass, jnp.zeros((6, 128), F32)], axis=0)
    lse_copy = send(LSN, lse_send, lse_recv, before)

    for c in stx:
        c.wait_recv()
    stz_send[...] = combine([stx_send[...]] + [stx_recv[j] for j in range(3)])
    stz = [send(STZ + j - 1, stz_send, stz_recv.at[j - 1], at_z(j)) for j in range(1, 16)]

    pltpu.make_async_copy(recv2, recv2, r_sem.at[A2A2]).wait()
    picked = mm(place[...], recv2[...].reshape(512, 128)).astype(BF)
    r8 = lax.broadcasted_iota(I32, (8, 128), 0)
    l8 = lax.broadcasted_iota(I32, (8, 128), 1)
    nbr_send[...] = nt(onehot((r8 == 0) & (l8 == 0)), picked)
    nbr = send(NBR, nbr_send, nbr_recv, before)
    sub128 = lax.broadcasted_iota(I32, (128, 128), 0)
    lane128 = lax.broadcasted_iota(I32, (128, 128), 1)
    moved = mm(picked, onehot(sub128 == lane128 + 1))
    nbr.wait_recv()
    moved += lax.dot_general(
        nbr_recv[...].astype(BF), onehot((r8 == 0) & (l8 == 127)),
        (((0,), (0,)), ((), ())), preferred_element_type=F32)
    lse_copy.wait_recv()
    l1 = lax.broadcasted_iota(I32, (1, 128), 1)

    def with_next(k):
        row = lse_send[k:k + 1, :]
        late = jnp.where(l1 == 127, pltpu.roll(lse_recv[k:k + 1, :], 127, 1), pltpu.roll(row, 127, 1))
        return jnp.concatenate([row, late], axis=1)

    t_lse = with_next(0)
    mass = with_next(1)
    probs[...] = jnp.exp(jnp.concatenate([picked.astype(F32), moved], axis=1) - t_lse)

    for c in stz:
        c.wait_recv()
    stat = combine([stz_send[...]] + [stz_recv[j] for j in range(15)])
    d_lse = stat[0:2] + jnp.log(stat[2:4])

    d_lse = jnp.concatenate([d_lse[0:1], d_lse[1:2]], axis=1)
    l256 = lax.broadcasted_iota(I32, (1, 256), 1)
    keep = jnp.where((l256 == 255) & (t == 7), 0.0, 64.0)
    low = logits[...].astype(BF).astype(F32)
    grads = (keep * (mass * jnp.exp(low - d_lse) - probs[...])).astype(BF)

    loss = jnp.sum(probs[...] * (d_lse - logits[...].astype(BF).astype(F32)), axis=0, keepdims=True)
    lox_send[...] = jnp.concatenate([loss[:, 0:128], loss[:, 128:]], axis=0)
    lox = [send(LOX + j - 1, lox_send, lox_recv.at[j - 1], at_x(j)) for j in range(1, 4)]

    def along_x_back(o):
        for j in range(1, 4):
            send(RSX + 3 * o + j - 1, rsx_send.at[o, lax.rem(x + j, 4)], rsx_recv.at[o, j - 1], at_x(j))

    first_z = []
    for o in (1, 3, 2, 0):
        bb = lax.rem(b + o, 4)

        def backward(i, c):
            cols = pl.ds(pl.multiple_of((i * 4 + bb) * 256, 256), 256)
            part = mm(head_t[cols, :], grads).reshape(4, 64, 256)
            wide[...] = part
            own[o, i] = wide[x, :, 0:128]
            for k in range(4):
                rsx_send[o, k, i] = part[k, :, 0:128].astype(BF)
                if o == 0:
                    own_z[k, i] = part[k, :, 128:256]
                else:
                    rsz_send[o - 1, k, i] = part[k, :, 128:256].astype(BF)
            return c

        lax.fori_loop(0, 4, backward, 0)
        if o == 1:
            first_z.append(send(RSZ, rsz_send.at[0], rsz_recv.at[0], at_z(1)))
        elif o == 3:
            first_z.append(send(RSZ + 1, rsz_send.at[2], rsz_recv.at[2], at_z(-1)))
        elif o == 2:
            for k, part in ((0, pl.ds(0, 2)), (1, pl.ds(2, 2))):
                first_z.append(send(RSZ + 2 + k, rsz_send.at[1, :, part], rsz_recv.at[1, :, part], at_z(4 * k - 2)))
        along_x_back(o)

    def loss_on():
        for c in lox:
            c.wait_recv()
        loz_send[...] = lox_send[...] + lox_recv[0] + lox_recv[1] + lox_recv[2]
        return [send(LOZ + j - 1, loz_send, loz_recv.at[j - 1], at_z(j)) for j in range(1, 16)]

    def loss_over(loz):
        for c in loz:
            c.wait_recv()
        whole = loz_send[...]
        for j in range(15):
            whole += loz_recv[j]
        los_send[...] = jnp.concatenate([whole, jnp.zeros((6, 128), F32)], axis=0)
        return send(LOS, los_send, los_recv, after)
    def summed(o, into):
        for j in range(1, 4):
            ref = rsx_recv.at[o, j - 1]
            copy(RSX + 3 * o + j - 1, ref, ref, at_x(1)).wait_recv()

        def add(i, c):
            into[i] = own[o, i] + rsx_recv[o, 0, i].astype(F32) + rsx_recv[o, 1, i].astype(F32) + rsx_recv[o, 2, i].astype(F32)
            return c

        lax.fori_loop(0, 4, add, 0)

    def far_copy(s, k):
        i = k + jnp.where(a <= k, 1, 0)
        j = lax.rem(i + 4 - a, 4)
        return send(RSS + 3 * s + j - 1, far_send.at[s, i], rss_recv.at[s, j - 1], ((i * 4 + b) * 4 + x, t))

    def to_far(s, first, parts):
        def add_last(i, c):
            rss_send[s, i] = first(i) + parts[0, i] + parts[1, i] + parts[2, i]
            return c

        lax.fori_loop(0, 4, add_last, 0)
        def narrow(i, c):
            far_send[s, i] = rss_send[s, i].astype(BF)
            return c

        lax.fori_loop(0, 4, narrow, 0)
        return [far_copy(s, k) for k in range(3)]

    loz = loss_on()
    near = []
    for o in (1, 3, 2):
        summed(o, rsn_send.at[o - 1])
        if o == 1:
            near.append(send(RSN, rsn_send.at[0], rsn_recv.at[0], at_z(1)))
        elif o == 3:
            near.append(send(RSN + 1, rsn_send.at[2], rsn_recv.at[2], at_z(-1)))
        else:
            for k, part in ((0, pl.ds(0, 2)), (1, pl.ds(2, 2))):
                near.append(send(RSN + 2 + k, rsn_send.at[1, part], rsn_recv.at[1, part], at_z(4 * k - 2)))
    for c in first_z:
        c.wait_recv()

    def add_z(i, c):
        for k in range(4):
            own_z[k, i] = (own_z[k, i] + rsz_recv[0, k, i].astype(F32) + rsz_recv[1, k, i].astype(F32)
                           + rsz_recv[2, k, i].astype(F32))
        return c

    lax.fori_loop(0, 4, add_z, 0)
    then_x = [send(RSY + j - 1, own_z.at[lax.rem(x + j, 4)], rsy_recv.at[j - 1], at_x(j)) for j in range(1, 4)]
    summed(0, rss_send.at[0])
    for c in near:
        c.wait_recv()
    far = to_far(0, lambda i: rss_send[0, i], rsn_recv)
    los = loss_over(loz)
    for c in then_x:
        c.wait_recv()
    far += to_far(1, lambda i: own_z[x, i], rsy_recv)

    los.wait_recv()
    here = los_send[...]
    other = los_recv[...]
    l8b = lax.broadcasted_iota(I32, (8, 128), 1)
    late = jnp.where(l8b == 0, jnp.where(t == 0, 0.0, pltpu.roll(other, 1, 1)), pltpu.roll(here, 1, 1))
    both = jnp.concatenate([here[0:1], late[1:2]], axis=0)
    l2 = lax.broadcasted_iota(I32, (2, 128), 1)
    for k in range(2):
        loss_out[:, k:k + 1] = jnp.sum(jnp.where(l2 == 2 * v + k, both, 0.0), axis=1, keepdims=True)

    for c in far:
        c.wait_recv()
    for s in range(2):
        grad_out[s] = (rss_send[s, a] + rss_recv[s, 0].astype(F32) + rss_recv[s, 1].astype(F32) + rss_recv[s, 2].astype(F32)).astype(BF)

    for c in sent:
        c.wait_send()
    for k, ref in ((A2A1, send1), (A2A2, send2)):
        most = ref.at[pl.ds(0, 63)]
        pltpu.make_async_copy(most, most, s_sem.at[k]).wait()


def on_device(target_logits, draft_hidden, draft_head, block_map):
    vm = pl.BlockSpec(memory_space=pltpu.VMEM)
    hbm = pl.BlockSpec(memory_space=pltpu.HBM)
    v = pltpu.VMEM
    tile = v((8, 128), F32)
    grad, loss = pl.pallas_call(
        kernel,
        name="draft_loss",
        out_shape=(jax.ShapeDtypeStruct((2, 64, 128), BF), jax.ShapeDtypeStruct((2, 2), F32)),
        in_specs=[hbm, hbm, hbm, hbm],
        out_specs=(vm, vm),
        scratch_shapes=[
            v((1, 256), I32), v((128, 2048), BF), v((512, 4096), BF), v((4096, 512), BF), v((4, 4, 4, 64, 256), BF),
            v((64, 16, 128), BF), v((64, 16, 128), BF), v((64, 8, 128), BF), v((64, 8, 128), BF),
            v((512, 1024), BF), v((512, 512), BF), v((512, 256), F32), v((512, 256), F32),
            tile, v((3, 8, 128), F32), tile, v((15, 8, 128), F32), tile, tile, v((8, 512), F32), v((8, 512), F32),
            v((4, 128), F32), v((3, 4, 128), F32), v((4, 128), F32), v((15, 4, 128), F32),
            v((2, 128), F32), v((3, 2, 128), F32), v((2, 128), F32), v((15, 2, 128), F32), tile, tile,
            v((4, 64, 256), F32), v((4, 4, 64, 128), F32), v((4, 4, 64, 128), F32),
            v((4, 4, 4, 64, 128), BF), v((4, 3, 4, 64, 128), BF),
            v((3, 4, 64, 128), F32), v((3, 4, 64, 128), F32),
            v((3, 4, 4, 64, 128), BF), v((3, 4, 4, 64, 128), BF), v((3, 4, 64, 128), F32),
            v((2, 4, 64, 128), F32), v((2, 4, 64, 128), BF), v((2, 3, 64, 128), BF),
            pltpu.SemaphoreType.DMA((N_SEMS,)), pltpu.SemaphoreType.DMA((N_SEMS,)),
        ],
        compiler_params=pltpu.CompilerParams(
            collective_id=0, has_side_effects=True, vmem_limit_bytes=62 * 1024 * 1024),
        cost_estimate=pl.CostEstimate(flops=2 ** 31, bytes_accessed=5 * 2 ** 20, transcendentals=2 ** 20),
    )(target_logits, draft_hidden.transpose(0, 2, 1), draft_head, block_map.reshape(1, 256))
    return grad.transpose(0, 2, 1), loss


def solution(mesh):
    return jax.shard_map(
        on_device,
        mesh=mesh,
        in_specs=(P("tok", "vocab"), P(None, "tok", "vocab"), P("vocab", None), P()),
        out_specs=(P(None, "tok", "vocab"), P(None, ("tok", "vocab"))),
        check_vma=False,
    )
```
